32 devices in a mesh: dp: 8 (over y, x, core), tensor: 4 (over z).
Axes of the slice: x: 2, y: 2, z: 4, core: 2. Of those that a mesh axis runs over, the one named last changes fastest.
Arguments:
- block_input: bfloat16 [2, 8192, 2048], P(None, ('dp', 'tensor')), may hold values from -6 to 6
- segment_ids: int32 [2, 8192], P(None, 'dp'), may hold values from 0 to 63, never falling along the last dimension, each value on 1 to 1024 neighbouring positions
- out_cotangent: bfloat16 [2, 8192, 2048], P(None, ('dp', 'tensor')), may hold values from -6 to 6
- norm1_gain: float32 [2048], replicated, may hold values from 0.5 to 1.5
- query_weight: bfloat16 [2048, 2048], P(None, 'tensor'), may hold values from -0.125 to 0.125
- key_weight: bfloat16 [2048, 2048], P(None, 'tensor'), may hold values from -0.125 to 0.125
- value_weight: bfloat16 [2048, 4096], P(None, 'tensor'), may hold values from -0.125 to 0.125
- gate_weight: bfloat16 [2048, 4096], P(None, 'tensor'), may hold values from -0.125 to 0.125
- decay_weight: bfloat16 [2048, 2, 16], P(None, None, 'tensor'), may hold values from -0.125 to 0.125
- conv_query: float32 [4, 2048], P(None, 'tensor'), may hold values from -2 to 2
- conv_key: float32 [4, 2048], P(None, 'tensor'), may hold values from -2 to 2
- conv_value: float32 [4, 4096], P(None, 'tensor'), may hold values from -2 to 2
- decay_log: float32 [16], P('tensor'), may hold values from -6 to 0
- decay_bias: float32 [16], P('tensor'), may hold values from -2 to 1
- output_gain: float32 [256], replicated, may hold values from 0.5 to 1.5
- output_weight: bfloat16 [4096, 2048], P('tensor'), may hold values from -0.1875 to 0.1875
- norm2_gain: float32 [2048], replicated, may hold values from 0.5 to 1.5
- ffn_gate: bfloat16 [2048, 5632], P(None, 'tensor'), may hold values from -0.125 to 0.125
- ffn_up: bfloat16 [2048, 5632], P(None, 'tensor'), may hold values from -0.125 to 0.125
- ffn_down: bfloat16 [5632, 2048], P('tensor'), may hold values from -0.109375 to 0.109375
Outputs:
- block_output: bfloat16 [2, 8192, 2048], P(None, ('dp', 'tensor'))
- input_grad: bfloat16 [2, 8192, 2048], P(None, ('dp', 'tensor'))
- grad_norm1_gain: float32 [2048], replicated
- grad_query_weight: float32 [2048, 2048], P(None, 'tensor')
- grad_key_weight: float32 [2048, 2048], P(None, 'tensor')
- grad_value_weight: float32 [2048, 4096], P(None, 'tensor')
- grad_gate_weight: float32 [2048, 4096], P(None, 'tensor')
- grad_decay_weight: float32 [2048, 2, 16], P(None, None, 'tensor')
- grad_conv_query: float32 [4, 2048], P(None, 'tensor')
- grad_conv_key: float32 [4, 2048], P(None, 'tensor')
- grad_conv_value: float32 [4, 4096], P(None, 'tensor')
- grad_decay_log: float32 [16], P('tensor')
- grad_decay_bias: float32 [16], P('tensor')
- grad_output_gain: float32 [256], replicated
- grad_output_weight: float32 [4096, 2048], P('tensor')
- grad_norm2_gain: float32 [2048], replicated
- grad_ffn_gate: float32 [2048, 5632], P(None, 'tensor')
- grad_ffn_up: float32 [2048, 5632], P(None, 'tensor')
- grad_ffn_down: float32 [5632, 2048], P('tensor')
The draws below stay inside these ranges and needn't reach their ends.
Inputs may be any that keep to these rules, and one draw needn't show every extreme that they name: `segment_ids`: ids never fall along a row; each document takes 1 to 1024 consecutive positions and one takes exactly 1024.
All inputs are finite; a program needn't handle non-finite values.
Results may differ from the reference program's by a relative error of at most 0.015.
Values may be sent and summed in bfloat16 or wider, within the bound.
No kernel may reach another device: no remote copies, remote signals or barrier semaphores. Data moves between devices by JAX's collectives and lax.ppermute only.
A program may use at most 768 MiB of HBM per device.

```python
import math
import jax
import jax.numpy as jnp
import numpy as np
from jax import lax

D = 2048
H = 16
DK = 128
DV = 256
FF = 5632
CONV = 4
SPAN = 64
MB = 2
SEQ = 1024
DOCS = 64
N_DP = 8


def shard_levels(stream_key, dims, split, low, high):
    def one(dim, blocks):
        steps = jax.random.uniform(jax.random.fold_in(jax.random.fold_in(stream_key, 6), dim), (blocks,), jnp.float32, low / len(split), high / len(split))
        return jnp.repeat(jnp.exp(steps), dims[dim] // blocks).reshape((-1,) + (1,) * (len(dims) - dim - 1))

    level = one(*split[0])
    for cut in split[1:]:
        level = level * one(*cut)
    return level


def profile(count, total, limit, slope):
    portions = [(1 << 20) // math.isqrt(rank ** slope) + 1 for rank in range(2, count + 1)]
    spare, holding = total - limit - (count - 1), [1] * (count - 1)
    while spare > 0:
        candidates = [i for i in range(count - 1) if holding[i] < limit]
        whole, budget = sum([portions[i] for i in candidates]), spare
        for i in candidates:
            addition = min(limit - holding[i], max(1, budget * portions[i] // whole), spare)
            holding[i] = holding[i] + addition
            spare = spare - addition
    return np.array([limit] + holding)


def ragged(key, count, total, reach, slope):
    if count == 2:
        one = jax.random.randint(key, (), max(1, total - reach), min(reach, total - 1) + 1)
        return jnp.stack([one, total - one])
    tallies = jnp.asarray(profile(count, total, reach, slope), jnp.int32)
    twos = (count - 1) // 2
    source_of, sink = tallies[1:1 + 2 * twos:2], tallies[2:2 + 2 * twos:2]
    room = jnp.minimum(source_of - 1, reach - sink)
    moved = jax.random.randint(jax.random.fold_in(key, 1), (twos,), 0, 1 << 20) % (room + 1)
    tallies = tallies.at[1:1 + 2 * twos:2].set(source_of - moved).at[2:2 + 2 * twos:2].set(sink + moved)
    return tallies[jax.random.permutation(jax.random.fold_in(key, 2), count)]


def bell_draw(rng, dims, deviation, limit, split=(), kind=jnp.bfloat16):
    values = deviation * jax.random.normal(rng, dims, jnp.float32)
    if split:
        values = values * shard_levels(rng, dims, split, -0.22, 0.18)
    return jnp.clip(values, -limit, limit).astype(kind)


def setup_inputs(seed: int = 0) -> dict:
    splits = jax.random.split(jax.random.key(seed), 21)
    block_input = bell_draw(splits[0], (MB, N_DP * SEQ, D), 1.0, 6.0, ((1, 32),))
    segment_ids = jax.vmap(lambda own: jnp.searchsorted(jnp.cumsum(ragged(own, DOCS, N_DP * SEQ, SEQ, 2)), jnp.arange(N_DP * SEQ), side="right"))(jax.random.split(splits[1], MB)).reshape((MB, N_DP * SEQ)).astype(jnp.int32)
    out_cotangent = bell_draw(splits[2], (MB, N_DP * SEQ, D), 1.0, 6.0, ((1, 32),))
    norm1_gain = jnp.clip(1.0 + 0.1 * jax.random.normal(splits[3], (D,), jnp.float32), 0.5, 1.5)
    query_weight = bell_draw(splits[4], (D, H * DK), D ** -0.5, 0.125, ((1, 4),))
    key_weight = bell_draw(splits[5], (D, H * DK), D ** -0.5, 0.125, ((1, 4),))
    value_weight = bell_draw(splits[6], (D, H * DV), D ** -0.5, 0.125, ((1, 4),))
    gate_weight = bell_draw(splits[7], (D, H * DV), D ** -0.5, 0.125, ((1, 4),))
    decay_weight = bell_draw(splits[8], (D, 2, H), D ** -0.5, 0.125, ((2, 4),))
    conv_query = bell_draw(splits[9], (CONV, H * DK), 0.5, 2.0, ((1, 4),), jnp.float32)
    conv_key = bell_draw(splits[10], (CONV, H * DK), 0.5, 2.0, ((1, 4),), jnp.float32)
    conv_value = bell_draw(splits[11], (CONV, H * DV), 0.5, 2.0, ((1, 4),), jnp.float32)
    decay_log = jnp.clip(-6.0 + 6.0 * jax.random.uniform(splits[12], (H,), jnp.float32) ** shard_levels(splits[12], (H,), ((0, 4),), -0.2, 0.2), -6.0, 0.0)
    decay_bias = jnp.clip(-2.0 + 3.0 * jax.random.uniform(splits[13], (H,), jnp.float32) ** shard_levels(splits[13], (H,), ((0, 4),), -0.2, 0.2), -2.0, 1.0)
    output_gain = jnp.clip(1.0 + 0.1 * jax.random.normal(splits[14], (DV,), jnp.float32), 0.5, 1.5)
    output_weight = bell_draw(splits[15], (H * DV, D), (H * DV // 4) ** -0.5, 0.1875, ((0, 4),))
    norm2_gain = jnp.clip(1.0 + 0.1 * jax.random.normal(splits[16], (D,), jnp.float32), 0.5, 1.5)
    ffn_gate = bell_draw(splits[17], (D, FF), D ** -0.5, 0.125, ((1, 4),))
    ffn_up = bell_draw(splits[18], (D, FF), D ** -0.5, 0.125, ((1, 4),))
    ffn_down = bell_draw(splits[19], (FF, D), (FF // 2) ** -0.5, 0.109375, ((0, 4),))
    return {"block_input": block_input, "segment_ids": segment_ids, "out_cotangent": out_cotangent, "norm1_gain": norm1_gain, "query_weight": query_weight, "key_weight": key_weight, "value_weight": value_weight, "gate_weight": gate_weight, "decay_weight": decay_weight, "conv_query": conv_query, "conv_key": conv_key, "conv_value": conv_value, "decay_log": decay_log, "decay_bias": decay_bias, "output_gain": output_gain, "output_weight": output_weight, "norm2_gain": norm2_gain, "ffn_gate": ffn_gate, "ffn_up": ffn_up, "ffn_down": ffn_down}


@jax.custom_vjp
def low(v):
    return lax.optimization_barrier(v.astype(jnp.bfloat16)).astype(jnp.float32)

@jax.custom_vjp
def low_back(v):
    return v

def low_keep(v):
    return (low(v), None)

def low_pass(kept, grad):
    return (grad,)

def back_keep(v):
    return (v, None)

def back_low(kept, grad):
    return (low(grad),)
low.defvjp(low_keep, low_pass)
low_back.defvjp(back_keep, back_low)

def rms_norm(values, gain_vec):
    return values * lax.rsqrt(lax.optimization_barrier(jnp.mean(values * values, axis=-1, keepdims=True)) + 1e-05) * gain_vec

def unit_rows(values):
    return values * lax.rsqrt(lax.optimization_barrier(jnp.sum(values * values, axis=-1, keepdims=True)) + 1e-06)

def causal_conv(values, weights, segments):
    length = values.shape[0]
    summed = weights[0] * values
    for offset in range(1, weights.shape[0]):
        shifted = jnp.concatenate([jnp.zeros((offset, values.shape[1]), jnp.float32), values[:length - offset]], axis=0)
        linked = jnp.concatenate([jnp.zeros((offset,), jnp.float32), (segments[offset:] == segments[:length - offset]).astype(jnp.float32)])
        summed = summed + weights[offset] * shifted * linked[:, None]
    return jax.nn.silu(summed)

def delta_rule(query_rows, key_rows, value_rows, beta_gate, decays, segments):
    length, head_count, key_size = query_rows.shape
    value_size = value_rows.shape[2]
    blocks = length // SPAN
    position = jnp.arange(SPAN)
    on_or_below = position[:, None] >= position[None, :]
    strict = position[:, None] > position[None, :]
    identity = jnp.eye(SPAN, dtype=jnp.float32)
    highest = lax.Precision.HIGHEST

    def advance(state_pair, inputs):
        memory, previous = state_pair
        q_blk, k_blk, v_blk, b_blk, d_blk, s_blk = inputs
        cum_decay = jnp.cumsum(d_blk, axis=0)
        same_doc = s_blk[:, None] == s_blk[None, :]
        log_gaps = cum_decay[:, None, :] - cum_decay[None, :, :]
        within = jnp.transpose(jnp.exp(jnp.where((same_doc & on_or_below)[:, :, None], log_gaps, -1e+30)), (2, 0, 1))
        before = jnp.transpose(jnp.exp(jnp.where((same_doc & strict)[:, :, None], log_gaps, -1e+30)), (2, 0, 1))
        carried = (s_blk == previous).astype(jnp.float32)
        growth = jnp.exp(cum_decay) * carried[:, None]
        key_key = jnp.einsum('ihd,jhd->hij', k_blk, k_blk, precision=highest)
        query_key = jnp.einsum('ihd,jhd->hij', q_blk, k_blk, precision=highest)
        key_state = jnp.einsum('ihd,hde->hie', k_blk, memory, precision=highest)
        query_state = jnp.einsum('ihd,hde->hie', q_blk, memory, precision=highest)
        beta_col = jnp.transpose(b_blk)[:, :, None]
        growth_col = jnp.transpose(growth)[:, :, None]
        system = identity + beta_col * key_key * before
        target = beta_col * (jnp.transpose(v_blk, (1, 0, 2)) - growth_col * key_state)
        solved = lax.linalg.triangular_solve(system, target, left_side=True, lower=True)
        output = growth_col * query_state + jnp.einsum('hij,hje->hie', query_key * within, solved, precision=highest)
        last_row = within[:, SPAN - 1, :]
        memory_next = growth[SPAN - 1][:, None, None] * memory + jnp.einsum('jhd,hj,hje->hde', k_blk, last_row, solved, precision=highest)
        return ((memory_next, s_blk[SPAN - 1]), jnp.transpose(output, (1, 0, 2)))

    def to_blocks(array):
        return array.reshape((blocks, SPAN) + array.shape[1:])
    start_pair = (jnp.zeros((head_count, key_size, value_size), jnp.float32), jnp.array(-1, dtype=jnp.int32))
    inputs = (to_blocks(query_rows), to_blocks(key_rows), to_blocks(value_rows), to_blocks(beta_gate), to_blocks(decays), to_blocks(segments))
    unused, outputs = lax.scan(advance, start_pair, inputs)
    return outputs.reshape(length, head_count, value_size)

def mixer_core(projected, segments, conv_query, conv_key, conv_value, decay_log, decay_bias, output_gain):
    length = projected.shape[0]
    head_count = decay_log.shape[0]
    qk_cols = conv_query.shape[1]
    v_cols = conv_value.shape[1]
    key_size = qk_cols // head_count
    value_size = v_cols // head_count
    query_rows = causal_conv(projected[:, :qk_cols], conv_query, segments).reshape(length, head_count, key_size)
    key_rows = causal_conv(projected[:, qk_cols:2 * qk_cols], conv_key, segments).reshape(length, head_count, key_size)
    value_rows = causal_conv(projected[:, 2 * qk_cols:2 * qk_cols + v_cols], conv_value, segments).reshape(length, head_count, value_size)
    gating = projected[:, 2 * qk_cols + v_cols:2 * qk_cols + 2 * v_cols].reshape(length, head_count, value_size)
    rate_col = 2 * qk_cols + 2 * v_cols
    rate_in = projected[:, rate_col:rate_col + head_count]
    beta_in = projected[:, rate_col + head_count:rate_col + 2 * head_count]
    query_rows = unit_rows(query_rows) * key_size ** (-0.5)
    key_rows = unit_rows(key_rows)
    beta_gate = jax.nn.sigmoid(beta_in)
    decays = -jnp.exp(decay_log) * jax.nn.softplus(rate_in + decay_bias)
    mixed_out = delta_rule(query_rows, key_rows, value_rows, beta_gate, decays, segments)
    mixed_out = rms_norm(mixed_out, output_gain) * jax.nn.silu(gating)
    return mixed_out.reshape(length, v_cols)

def dot_high(left, right):
    return jnp.dot(left.astype(jnp.float32), right.astype(jnp.float32), precision=lax.Precision.HIGHEST, preferred_element_type=jnp.float32)

def block_forward(inputs, segments, params):
    norm1_gain, query_weight, key_weight, value_weight, gate_weight, decay_weight, conv_query, conv_key, conv_value, decay_log, decay_bias, output_gain, output_weight, norm2_gain, ffn_gate, ffn_up, ffn_down = params
    seq_count, length, width = inputs.shape
    flat_rows = inputs.reshape(seq_count * length, width)
    normed = low(rms_norm(flat_rows, norm1_gain))
    weights_all = jnp.concatenate([query_weight, key_weight, value_weight, gate_weight, decay_weight.reshape(width, -1)], axis=1)
    projected = low_back(dot_high(normed, weights_all)).reshape(seq_count, length, -1)

    def one_sequence(proj_rows, seg_rows):
        return mixer_core(proj_rows, seg_rows, conv_query, conv_key, conv_value, decay_log, decay_bias, output_gain)
    mixed_out = jax.vmap(one_sequence)(projected, segments)
    rounded = low(mixed_out.reshape(seq_count * length, -1))
    branch = low_back(dot_high(rounded, output_weight))
    residual = flat_rows + branch
    ffn_input = low(rms_norm(residual, norm2_gain))
    gate_pre = low_back(dot_high(ffn_input, ffn_gate))
    up_pre = low_back(dot_high(ffn_input, ffn_up))
    hidden = low(jax.nn.silu(gate_pre) * up_pre)
    ffn_out = low_back(dot_high(hidden, ffn_down))
    return (residual + ffn_out).reshape(seq_count, length, width)

def reference(block_input, segment_ids, out_cotangent, norm1_gain, query_weight, key_weight, value_weight, gate_weight, decay_weight, conv_query, conv_key, conv_value, decay_log, decay_bias, output_gain, output_weight, norm2_gain, ffn_gate, ffn_up, ffn_down):
    seq_total = MB * N_DP
    seq_group = math.gcd(seq_total, max(1, 4096 // SEQ))
    shape_in = (seq_total // seq_group, seq_group, SEQ, D)
    inputs = block_input.astype(jnp.float32).reshape(shape_in)
    segments = segment_ids.reshape(seq_total // seq_group, seq_group, SEQ)
    cotangent = out_cotangent.astype(jnp.float32).reshape(shape_in)
    params = tuple((weight.astype(jnp.float32) for weight in (norm1_gain, query_weight, key_weight, value_weight, gate_weight, decay_weight, conv_query, conv_key, conv_value, decay_log, decay_bias, output_gain, output_weight, norm2_gain, ffn_gate, ffn_up, ffn_down)))
    runner = jax.checkpoint(block_forward)

    def forward(inputs_all, params_all):
        return lax.map(lambda paired: runner(paired[0], paired[1], params_all), (inputs_all, segments))
    outputs, backward = jax.vjp(forward, inputs, params)
    input_grad, grads = backward(cotangent)
    out_shape = (MB, N_DP * SEQ, D)
    return (outputs.reshape(out_shape).astype(jnp.bfloat16), input_grad.reshape(out_shape).astype(jnp.bfloat16), grads[0], grads[1], grads[2], grads[3], grads[4], grads[5], grads[6], grads[7], grads[8], grads[9], grads[10], grads[11], grads[12], grads[13], grads[14], grads[15], grads[16])
```

```python
import functools
import jax
import jax.numpy as jnp
from jax import lax
from jax.experimental import pallas as pl
from jax.experimental.pallas import tpu as pltpu
from jax.sharding import PartitionSpec as P

SPAN = 64
LANES = 128
HALO = 8
DK = 128
DV = 256
LOW = jnp.bfloat16
F32 = jnp.float32


def mm(left, right):
    return jnp.dot(left.astype(LOW), right.astype(LOW), preferred_element_type=F32)


def mm_tb(left, right):
    return lax.dot_general(
        left.astype(LOW), right.astype(LOW), (((1,), (1,)), ((), ())), preferred_element_type=F32
    )


def mm_ta(left, right):
    return lax.dot_general(
        left.astype(LOW), right.astype(LOW), (((0,), (0,)), ((), ())), preferred_element_type=F32
    )


def mm_exact(left, right):
    return jnp.dot(left, right, precision=lax.Precision.HIGHEST, preferred_element_type=F32)


def grid_pair(rows, cols):
    return (
        lax.broadcasted_iota(jnp.int32, (rows, cols), 0),
        lax.broadcasted_iota(jnp.int32, (rows, cols), 1),
    )


def lower_inverses(strict_lowers):
    row, col = grid_pair(SPAN, SPAN)
    eye = (row == col).astype(F32)
    size = 1
    inverses = None
    while size < SPAN:
        fresh = (row // (2 * size) == col // (2 * size)) & (row // size != col // size)
        parts = [jnp.where(fresh, lower, 0.0) for lower in strict_lowers]
        if size == 1:
            inverses = [eye - part for part in parts]
        else:
            lows = [inverse.astype(LOW) for inverse in inverses]
            firsts = [mm(part, low) for part, low in zip(parts, lows)]
            inverses = [
                inverse - mm(low, first) for inverse, low, first in zip(inverses, lows, firsts)
            ]
        size *= 2
    return inverses


def gates(small, params):
    rate = small + params[1:2, :]
    soft = jnp.maximum(rate, 0.0) + jnp.log1p(jnp.exp(-jnp.abs(rate)))
    return rate, params[0:1, :] * soft, jax.nn.sigmoid(small)


def decay_tables(decay, aux):
    row, col = grid_pair(SPAN, SPAN)
    running = mm_exact((row >= col).astype(F32), decay)
    lane = lax.broadcasted_iota(jnp.int32, (SPAN, LANES), 1)
    flipped = jnp.transpose(jnp.where(lane == LANES - 1, aux[:, 0:1], running))
    growth = jnp.exp(running) * aux[:, 1:2]
    tail = jnp.exp(jnp.where(aux[:, 2:3] > 0.0, running[SPAN - 1 : SPAN, :] - running, -1e30))
    keep = (aux[:, 0:1] == flipped[LANES - 1 : LANES, :]) & (row >= col)
    return running, flipped, growth, tail, keep


def conv_in(window_ref, start, width, taps, aux):
    total = taps[0:1, start : start + width] * window_ref[HALO : HALO + SPAN, start : start + width]
    for offset in range(1, 4):
        shifted = window_ref[HALO - offset : HALO - offset + SPAN, start : start + width]
        total = total + taps[offset : offset + 1, start : start + width] * (
            shifted * aux[:, 2 + offset : 3 + offset]
        )
    return total


def unit(values):
    return values * lax.rsqrt(jnp.sum(values * values, axis=-1, keepdims=True) + 1e-06)


def forward_kernel(
    heads, proj_ref, halo_ref, aux_ref, taps_ref, params_ref, gain_ref,
    mixed_ref, delta_ref, solved_ref, inverse_ref, entry_ref, memory_ref, window_ref,
):
    qk_cols, v_cols = heads * DK, heads * DV
    gate_at = 2 * qk_cols + v_cols
    small_at = gate_at + v_cols

    @pl.when(pl.program_id(0) == 0)
    def _():
        memory_ref[...] = jnp.zeros_like(memory_ref)

    window_ref[0:HALO, :] = halo_ref[:, 0:gate_at]
    window_ref[HALO : HALO + SPAN, :] = proj_ref[:, 0:gate_at]
    aux = aux_ref[...]
    taps = taps_ref[...]
    _, decay, writes = gates(proj_ref[:, small_at : small_at + LANES], params_ref[...])
    running, flipped, growth, tail, keep = decay_tables(decay, aux)
    row, col = grid_pair(SPAN, SPAN)
    each = range(heads)
    queries = [
        unit(jax.nn.silu(conv_in(window_ref, h * DK, DK, taps, aux))) * DK ** (-0.5) for h in each
    ]
    keys = [
        unit(jax.nn.silu(conv_in(window_ref, qk_cols + h * DK, DK, taps, aux))) for h in each
    ]
    boths = [
        jnp.concatenate([query.astype(LOW), key.astype(LOW)], axis=0)
        for query, key in zip(queries, keys)
    ]
    scores = [mm_tb(both, both[SPAN:]) for both in boths]
    withins = [
        jnp.exp(jnp.where(keep, running[:, h : h + 1] - flipped[h : h + 1, :], -1e30))
        for h in each
    ]
    betas = [writes[:, heads + h : heads + h + 1] for h in each]
    grows = [growth[:, h : h + 1] for h in each]
    inverses = lower_inverses(
        [
            betas[h] * scores[h][SPAN:] * jnp.where(row > col, withins[h], 0.0)
            for h in each
        ]
    )
    inverses = [inverse.astype(LOW) for inverse in inverses]
    memories = [memory_ref[h] for h in each]
    lows = [memory.astype(LOW) for memory in memories]
    reads = [mm(both, low) for both, low in zip(boths, lows)]
    values = [
        jax.nn.silu(conv_in(window_ref, 2 * qk_cols + h * DV, DV, taps, aux)) for h in each
    ]
    targets = [betas[h] * (values[h] - grows[h] * reads[h][SPAN:]) for h in each]
    solveds = [mm(inverses[h], targets[h]).astype(LOW) for h in each]
    updates = [mm_ta(tail[:, h : h + 1] * keys[h], solveds[h]) for h in each]
    deltas = [
        grows[h] * reads[h][:SPAN] + mm(scores[h][:SPAN] * withins[h], solveds[h]) for h in each
    ]
    for h in each:
        entry_ref[0, h] = lows[h]
        inverse_ref[0, h] = inverses[h]
        memory_ref[h] = grows[h][SPAN - 1 : SPAN, :] * memories[h] + updates[h]
        cols = slice(h * DV, (h + 1) * DV)
        delta = deltas[h]
        solved_ref[:, cols] = solveds[h]
        delta_ref[:, cols] = delta
        scaled = delta * lax.rsqrt(jnp.mean(delta * delta, axis=-1, keepdims=True) + 1e-05)
        gate = proj_ref[:, gate_at + h * DV : gate_at + (h + 1) * DV]
        mixed_ref[:, cols] = (scaled * gain_ref[0:1, :] * jax.nn.silu(gate)).astype(LOW)


def silu_back(values, grad):
    sig = jax.nn.sigmoid(values)
    return grad * sig * (1.0 + values * (1.0 - sig))


def fold(values):
    total = values[0:8]
    for part in range(1, values.shape[0] // 8):
        total = total + values[8 * part : 8 * part + 8]
    return total


def backward_kernel(
    heads, proj_ref, halo_ref, aux_ref, taps_ref, params_ref, gain_ref,
    delta_ref, solved_ref, inverse_ref, entry_ref, grad_ref,
    dproj_ref, dtaps_ref, dsmall_ref, dgain_ref, dmemory_ref, window_ref, later_ref,
):
    qk_cols, v_cols = heads * DK, heads * DV
    gate_at = 2 * qk_cols + v_cols
    small_at = gate_at + v_cols

    @pl.when(pl.program_id(0) == 0)
    def _():
        dmemory_ref[...] = jnp.zeros_like(dmemory_ref)
        later_ref[...] = jnp.zeros_like(later_ref)
        dtaps_ref[...] = jnp.zeros_like(dtaps_ref)
        dsmall_ref[...] = jnp.zeros_like(dsmall_ref)
        dgain_ref[...] = jnp.zeros_like(dgain_ref)

    window_ref[0:HALO, :] = halo_ref[:, 0:gate_at]
    window_ref[HALO : HALO + SPAN, :] = proj_ref[:, 0:gate_at]
    later_ref[SPAN : SPAN + HALO, :] = later_ref[0:HALO, :]
    aux = aux_ref[...]
    taps = taps_ref[...]
    small = proj_ref[:, small_at : small_at + LANES]
    rate, decay, writes = gates(small, params_ref[...])
    running, flipped, growth, tail, keep = decay_tables(decay, aux)
    row, col = grid_pair(SPAN, SPAN)
    lane = lax.broadcasted_iota(jnp.int32, (SPAN, LANES), 1)
    upper = (row <= col).astype(F32)
    behind = (row > col).astype(F32)
    dbeta_all = jnp.zeros((SPAN, LANES), F32)
    arrive_all = jnp.zeros((SPAN, LANES), F32)
    leave_all = jnp.zeros((SPAN, LANES), F32)
    direct_all = jnp.zeros((SPAN, LANES), F32)

    def conv_back(pre, grad, start, width):
        dpre = silu_back(pre, grad)
        later_ref[0:SPAN, start : start + width] = dpre
        total = taps[0:1, start : start + width] * dpre
        base = window_ref[HALO : HALO + SPAN, start : start + width]
        dtaps_ref[0:8, start : start + width] += fold(dpre * base)
        for offset in range(1, 4):
            ahead = later_ref[offset : offset + SPAN, start : start + width]
            total = total + taps[offset : offset + 1, start : start + width] * (
                ahead * aux[:, 5 + offset : 6 + offset]
            )
            shifted = window_ref[HALO - offset : HALO - offset + SPAN, start : start + width]
            dtaps_ref[8 * offset : 8 * offset + 8, start : start + width] += fold(
                dpre * (shifted * aux[:, 2 + offset : 3 + offset])
            )
        dproj_ref[:, start : start + width] = total.astype(LOW)

    each = range(heads)
    values_at = [slice(h * DV, (h + 1) * DV) for h in each]
    ddeltas = []
    for h in each:
        delta = delta_ref[:, values_at[h]]
        scale = lax.rsqrt(jnp.mean(delta * delta, axis=-1, keepdims=True) + 1e-05)
        scaled = delta * scale
        gate = proj_ref[:, gate_at + h * DV : gate_at + (h + 1) * DV]
        gsig = jax.nn.sigmoid(gate)
        dmixed = grad_ref[:, values_at[h]]
        gain = gain_ref[0:1, :]
        dproj_ref[:, gate_at + h * DV : gate_at + (h + 1) * DV] = (
            dmixed * scaled * gain * gsig * (1.0 + gate * (1.0 - gsig))
        ).astype(LOW)
        dnormed = dmixed * (gate * gsig)
        dgain_ref[...] += fold(dnormed * scaled)
        dnormed = dnormed * gain
        ddelta = scale * (
            dnormed - scaled * jnp.mean(scaled * dnormed, axis=-1, keepdims=True)
        )
        ddeltas.append(ddelta.astype(LOW))
    q_pres = [conv_in(window_ref, h * DK, DK, taps, aux) for h in each]
    k_pres = [conv_in(window_ref, qk_cols + h * DK, DK, taps, aux) for h in each]
    q_acts = [jax.nn.silu(pre) for pre in q_pres]
    k_acts = [jax.nn.silu(pre) for pre in k_pres]
    q_scales = [
        lax.rsqrt(jnp.sum(act * act, axis=-1, keepdims=True) + 1e-06) for act in q_acts
    ]
    k_scales = [
        lax.rsqrt(jnp.sum(act * act, axis=-1, keepdims=True) + 1e-06) for act in k_acts
    ]
    q_units = [act * scale for act, scale in zip(q_acts, q_scales)]
    keys = [act * scale for act, scale in zip(k_acts, k_scales)]
    queries = [unit_row * DK ** (-0.5) for unit_row in q_units]
    betas = [writes[:, heads + h : heads + h + 1] for h in each]
    grows = [growth[:, h : h + 1] for h in each]
    fades = [tail[:, h : h + 1] for h in each]
    withins = [
        jnp.exp(jnp.where(keep, running[:, h : h + 1] - flipped[h : h + 1, :], -1e30))
        for h in each
    ]
    key_lows = [key.astype(LOW) for key in keys]
    boths = [
        jnp.concatenate([query.astype(LOW), low], axis=0) for query, low in zip(queries, key_lows)
    ]
    scores = [mm_tb(both, low) for both, low in zip(boths, key_lows)]
    solveds = [solved_ref[:, values_at[h]] for h in each]
    entries = [entry_ref[0, h] for h in each]
    dmemories = [dmemory_ref[h] for h in each]
    dmemory_lows = [dmemory.astype(LOW) for dmemory in dmemories]
    leaving = [mm(low, dlow) for low, dlow in zip(key_lows, dmemory_lows)]
    dsolveds = [
        mm_ta(scores[h][:SPAN] * withins[h], ddeltas[h]) + fades[h] * leaving[h] for h in each
    ]
    dtargets = [mm_ta(inverse_ref[0, h], dsolveds[h]) for h in each]
    pairs = [
        jnp.concatenate([ddeltas[h], dtargets[h].astype(LOW)], axis=0) for h in each
    ]
    factors = [
        jnp.concatenate(
            [
                (grows[h] * queries[h]).astype(LOW),
                (-(betas[h] * grows[h]) * keys[h]).astype(LOW),
            ],
            axis=0,
        )
        for h in each
    ]
    flows = [mm_ta(factor, pair) for factor, pair in zip(factors, pairs)]
    carries = []
    for h in each:
        last = grows[h][SPAN - 1 : SPAN, :]
        carries.append(
            last * jnp.sum(dmemories[h] * entries[h].astype(F32), keepdims=True)
        )
        dmemory_ref[h] = last * dmemories[h] + flows[h]
    on_solveds = [mm_tb(pair, solved) for pair, solved in zip(pairs, solveds)]
    on_entries = [mm_tb(pair, entry) for pair, entry in zip(pairs, entries)]
    dkey_leaves = [
        fades[h] * mm_tb(solveds[h], dmemory_lows[h]) for h in each
    ]
    dscores = [on_solveds[h][:SPAN] * withins[h] for h in each]
    dsystems = [
        -on_solveds[h][SPAN:] * jnp.where(row > col, withins[h], 0.0) for h in each
    ]
    dsystem_betas = [betas[h] * dsystems[h] for h in each]
    duos = [
        jnp.concatenate([dscores[h].astype(LOW), dsystem_betas[h].astype(LOW)], axis=0)
        for h in each
    ]
    forths = [mm(duo, low) for duo, low in zip(duos, key_lows)]
    backs = [mm_ta(duo, both) for duo, both in zip(duos, boths)]
    spreads = [
        mm(upper, dscores[h] * scores[h][:SPAN] + dsystem_betas[h] * scores[h][SPAN:])
        for h in each
    ]
    for h in each:
        q_at, k_at, v_at = h * DK, qk_cols + h * DK, 2 * qk_cols + h * DV
        key, query, beta = keys[h], queries[h], betas[h]
        dquery_far = grows[h] * on_entries[h][:SPAN]
        dkey_far = grows[h] * on_entries[h][SPAN:]
        dquery = dquery_far + forths[h][:SPAN]
        dkey = forths[h][SPAN:] + backs[h] - beta * dkey_far + dkey_leaves[h]
        v_pre = conv_in(window_ref, v_at, DV, taps, aux)
        value = jax.nn.silu(v_pre)
        key_far = jnp.sum(key * dkey_far, axis=-1, keepdims=True)
        dbeta = (
            jnp.sum(dtargets[h] * value, axis=-1, keepdims=True)
            - key_far
            + jnp.sum(dsystems[h] * scores[h][SPAN:], axis=-1, keepdims=True)
        )
        arrive = jnp.sum(query * dquery_far, axis=-1, keepdims=True) - beta * key_far
        leave = jnp.sum(key * dkey_leaves[h], axis=-1, keepdims=True)
        direct = jnp.sum(spreads[h] * behind, axis=-1, keepdims=True) + carries[h]
        dbeta_all = jnp.where(lane == heads + h, dbeta, dbeta_all)
        arrive_all = jnp.where(lane == h, arrive, arrive_all)
        leave_all = jnp.where(lane == h, leave, leave_all)
        direct_all = jnp.where(lane == h, direct, direct_all)
        dq_unit = dquery * DK ** (-0.5)
        dq_act = q_scales[h] * (
            dq_unit - q_units[h] * jnp.sum(q_units[h] * dq_unit, axis=-1, keepdims=True)
        )
        dk_act = k_scales[h] * (dkey - key * jnp.sum(key * dkey, axis=-1, keepdims=True))
        conv_back(q_pres[h], dq_act, q_at, DK)
        conv_back(k_pres[h], dk_act, k_at, DK)
        conv_back(v_pre, beta * dtargets[h], v_at, DV)

    ddecay = direct_all + mm_exact(upper, arrive_all) + mm_exact(behind, leave_all)
    drate = ddecay * params_ref[0:1, :] * jax.nn.sigmoid(rate)
    dsmall_ref[0:8, :] += fold(ddecay * decay)
    dsmall_ref[8:16, :] += fold(drate)
    dproj_ref[:, small_at : small_at + LANES] = (
        drate + dbeta_all * writes * (1.0 - writes)
    ).astype(LOW)


def whole(shape):
    return pl.BlockSpec(shape, lambda step: (0,) * len(shape))


def mixer_forward(projected, aux, taps, params, gain, heads):
    rows, width = projected.shape
    v_cols = heads * DV
    conv_cols = taps.shape[1]
    blocks = rows // SPAN
    tall = SPAN // HALO
    return pl.pallas_call(
        functools.partial(forward_kernel, heads),
        grid=(blocks,),
        in_specs=[
            pl.BlockSpec((SPAN, width), lambda c: (c, 0)),
            pl.BlockSpec((HALO, width), lambda c: (jnp.maximum(c * tall - 1, 0), 0)),
            pl.BlockSpec((SPAN, LANES), lambda c: (c, 0)),
            whole(taps.shape),
            whole(params.shape),
            whole((8, DV)),
        ],
        out_specs=[
            pl.BlockSpec((SPAN, v_cols), lambda c: (c, 0)),
            pl.BlockSpec((SPAN, v_cols), lambda c: (c, 0)),
            pl.BlockSpec((SPAN, v_cols), lambda c: (c, 0)),
            pl.BlockSpec((1, heads, SPAN, SPAN), lambda c: (c, 0, 0, 0)),
            pl.BlockSpec((1, heads, DK, DV), lambda c: (c, 0, 0, 0)),
        ],
        out_shape=[
            jax.ShapeDtypeStruct((rows, v_cols), LOW),
            jax.ShapeDtypeStruct((rows, v_cols), F32),
            jax.ShapeDtypeStruct((rows, v_cols), LOW),
            jax.ShapeDtypeStruct((blocks, heads, SPAN, SPAN), LOW),
            jax.ShapeDtypeStruct((blocks, heads, DK, DV), LOW),
        ],
        scratch_shapes=[
            pltpu.VMEM((heads, DK, DV), F32),
            pltpu.VMEM((SPAN + HALO, conv_cols), F32),
        ],
        compiler_params=pltpu.CompilerParams(vmem_limit_bytes=40 << 20),
        cost_estimate=pl.CostEstimate(
            flops=rows, bytes_accessed=rows, transcendentals=0
        ),
        name="mixer_forward",
    )(projected, projected, aux, taps, params, gain)


def mixer_backward(projected, aux, taps, params, gain, saved, grad, heads):
    delta, solved, inverse, entry = saved
    rows, width = projected.shape
    v_cols = heads * DV
    conv_cols = taps.shape[1]
    blocks = rows // SPAN
    tall = SPAN // HALO
    last = blocks - 1
    return pl.pallas_call(
        functools.partial(backward_kernel, heads),
        grid=(blocks,),
        in_specs=[
            pl.BlockSpec((SPAN, width), lambda c: (last - c, 0)),
            pl.BlockSpec((HALO, width), lambda c: (jnp.maximum((last - c) * tall - 1, 0), 0)),
            pl.BlockSpec((SPAN, LANES), lambda c: (last - c, 0)),
            whole(taps.shape),
            whole(params.shape),
            whole((8, DV)),
            pl.BlockSpec((SPAN, v_cols), lambda c: (last - c, 0)),
            pl.BlockSpec((SPAN, v_cols), lambda c: (last - c, 0)),
            pl.BlockSpec((1, heads, SPAN, SPAN), lambda c: (last - c, 0, 0, 0)),
            pl.BlockSpec((1, heads, DK, DV), lambda c: (last - c, 0, 0, 0)),
            pl.BlockSpec((SPAN, v_cols), lambda c: (last - c, 0)),
        ],
        out_specs=[
            pl.BlockSpec((SPAN, width), lambda c: (last - c, 0)),
            whole((32, conv_cols)),
            whole((16, LANES)),
            whole((8, DV)),
        ],
        out_shape=[
            jax.ShapeDtypeStruct((rows, width), LOW),
            jax.ShapeDtypeStruct((32, conv_cols), F32),
            jax.ShapeDtypeStruct((16, LANES), F32),
            jax.ShapeDtypeStruct((8, DV), F32),
        ],
        scratch_shapes=[
            pltpu.VMEM((heads, DK, DV), F32),
            pltpu.VMEM((SPAN + HALO, conv_cols), F32),
            pltpu.VMEM((SPAN + HALO, conv_cols), F32),
        ],
        compiler_params=pltpu.CompilerParams(vmem_limit_bytes=48 << 20),
        cost_estimate=pl.CostEstimate(
            flops=rows, bytes_accessed=rows, transcendentals=0
        ),
        name="mixer_backward",
    )(projected, projected, aux, taps, params, gain, delta, solved, inverse, entry, grad)


def token_tables(segments):
    rows = segments.shape[0]
    seg = segments.astype(F32)
    blocked = seg.reshape(rows // SPAN, SPAN)
    ends = blocked[:, SPAN - 1]
    before = jnp.concatenate([jnp.full((1,), -1.0, F32), ends[:-1]])
    columns = [
        seg,
        (blocked == before[:, None]).astype(F32).reshape(rows),
        (blocked == ends[:, None]).astype(F32).reshape(rows),
    ]
    links = [(seg[offset:] == seg[:-offset]).astype(F32) for offset in range(1, 4)]
    columns += [jnp.pad(link, (offset, 0)) for offset, link in enumerate(links, 1)]
    columns += [jnp.pad(link, (0, offset)) for offset, link in enumerate(links, 1)]
    return jnp.pad(jnp.stack(columns, axis=1), ((0, 0), (0, LANES - len(columns))))


def rms_forward(values, gain_vec):
    scale = lax.rsqrt(jnp.mean(values * values, axis=-1, keepdims=True) + 1e-05)
    return values * scale * gain_vec


def rms_backward(values, gain_vec, grad):
    scale = lax.rsqrt(jnp.mean(values * values, axis=-1, keepdims=True) + 1e-05)
    scaled = values * scale
    inner = grad * gain_vec
    back = scale * (inner - scaled * jnp.mean(scaled * inner, axis=-1, keepdims=True))
    return back, jnp.sum(grad * scaled, axis=0)


def dot(left, right):
    return jnp.dot(left, right, preferred_element_type=F32)


def contract_rows(left, right):
    return lax.dot_general(
        left, right, (((0,), (0,)), ((), ())), preferred_element_type=F32
    )


def contract_cols(left, right):
    return lax.dot_general(
        left, right, (((1,), (1,)), ((), ())), preferred_element_type=F32
    )


def gather(rows):
    return lax.all_gather(rows, "tensor", axis=0, tiled=True)


def scatter(rows):
    return lax.psum_scatter(
        rows.astype(LOW), "tensor", scatter_dimension=0, tiled=True
    ).astype(F32)


def after(values, first):
    return lax.optimization_barrier((values, first))[0]


def make_body(parts, replicas):
    near = parts // 2
    teams = [list(range(near)), list(range(near, parts))]
    swap = [(i, i ^ 1) for i in range(parts)]
    across = [(i, (i + near) % parts) for i in range(parts)]

    def team_exchange(rows):
        if near == 2:
            return lax.ppermute(rows, "tensor", swap)
        return lax.all_gather(rows, "tensor", axis=0, tiled=True, axis_index_groups=teams)

    def team_join(rows, others):
        return jnp.concatenate([rows, others], axis=0) if near == 2 else others

    def team_gather(rows):
        return team_join(rows, team_exchange(rows))

    def team_scatter(rows):
        if near == 2:
            half = rows.shape[0] // 2
            return rows[:half] + lax.ppermute(rows[half:].astype(LOW), "tensor", swap).astype(F32)
        return lax.psum_scatter(
            rows.astype(LOW), "tensor", scatter_dimension=0, tiled=True, axis_index_groups=teams
        ).astype(F32)

    def scatter_direct(rows):
        size = rows.shape[0] // parts
        place = lax.axis_index("tensor")

        def part(hop):
            index = lax.rem(place + hop, parts)
            return lax.dynamic_slice_in_dim(rows, index * size, size)

        total = part(0).astype(F32)
        for hop in range(1, parts):
            pairs = [(i, (i + hop) % parts) for i in range(parts)]
            total = total + lax.ppermute(part(hop).astype(LOW), "tensor", pairs).astype(F32)
        return total

    def own_piece(matrix):
        rows = matrix.shape[0] // replicas
        return lax.dynamic_slice_in_dim(matrix, lax.axis_index("dp") * rows, rows)

    def spread(piece):
        return lax.all_gather(piece, "dp", axis=0, tiled=True)

    def body(
        block_input,
        segment_ids,
        out_cotangent,
        norm1_gain,
        query_weight,
        key_weight,
        value_weight,
        gate_weight,
        decay_weight,
        conv_query,
        conv_key,
        conv_value,
        decay_log,
        decay_bias,
        output_gain,
        output_weight,
        norm2_gain,
        ffn_gate,
        ffn_up,
        ffn_down,
    ):
        batch_count, slice_rows, width = block_input.shape
        heads = decay_log.shape[0]
        qk_cols = query_weight.shape[1]
        v_cols = value_weight.shape[1]
        ffn_cols = ffn_gate.shape[1]
        batches = range(batch_count)
        x_rows = [block_input[b].astype(F32) for b in batches]
        cot_rows = [out_cotangent[b] for b in batches]
        first_rows = [rms_forward(x_rows[b], norm1_gain).astype(LOW) for b in batches]
        ffn_both = jnp.concatenate([ffn_gate, ffn_up], axis=1)
        proj_all = jnp.concatenate(
            [
                query_weight,
                key_weight,
                value_weight,
                gate_weight,
                decay_weight.reshape(width, 2 * heads),
                jnp.zeros((width, LANES - 2 * heads), LOW),
            ],
            axis=1,
        )
        taps = jnp.pad(
            jnp.concatenate([conv_query, conv_key, conv_value], axis=1), ((0, 4), (0, 0))
        )
        params = jnp.pad(
            jnp.stack([-jnp.exp(decay_log), decay_bias]), ((0, 6), (0, LANES - heads))
        )
        gain = jnp.broadcast_to(output_gain, (8, output_gain.shape[0]))
        aux = [token_tables(segment_ids[b]) for b in batches]

        normed, projs, mixeds, saveds, branches, cot_full = [], [], [], [], [], []
        pieces = [own_piece(ffn_both), own_piece(ffn_down)]
        far = None
        for b in batches:
            rows = first_rows[b]
            if b > 0:
                rows = after(rows, normed[b - 1])
            normed.append(gather(rows))
        pieces = [
            lax.ppermute(after(piece, proj_all), "tensor", across) for piece in pieces
        ]
        far = [spread(piece) for piece in pieces]
        cot_pairs = [team_exchange(after(rows, pieces)) for rows in cot_rows]
        cot_full = [team_join(cot_rows[b], cot_pairs[b]) for b in batches]
        for b in batches:
            rows = after(normed[b], branches[b - 1]) if b > 0 else normed[b]
            projected = dot(rows, proj_all)
            mixed, *saved = mixer_forward(projected, aux[b], taps, params, gain, heads)
            mixed = after(mixed, pieces if b == 0 else cot_pairs)
            projs.append(projected)
            mixeds.append(mixed)
            saveds.append(saved)
            branches.append(dot(mixed, output_weight).astype(LOW))
        last = branches[-1]
        branches = [scatter(rows) for rows in branches]

        near_weights, far_weights = (ffn_both, ffn_down), tuple(far)

        def ffn_half(rows, cot, weights):
            both, down = weights
            gate_up = dot(rows, both)
            gate_pre, up_pre = gate_up[:, :ffn_cols], gate_up[:, ffn_cols:]
            sig = jax.nn.sigmoid(gate_pre)
            hidden = (gate_pre * sig * up_pre).astype(LOW)
            dhidden = contract_cols(cot, down)
            dgate = dhidden * up_pre * sig * (1.0 + gate_pre * (1.0 - sig))
            dup = dhidden * (gate_pre * sig)
            return hidden, jnp.concatenate([dgate, dup], axis=1).astype(LOW)

        residuals = [None] * batch_count
        ffn_full = [None] * batch_count
        hiddens = [None] * batch_count
        dboths = [None] * batch_count
        partial_in = [None] * batch_count
        partial_out = [None] * batch_count
        dresiduals = [None] * batch_count
        dbranch = [None] * batch_count
        gain2 = []

        def enter(b, behind):
            residuals[b] = x_rows[b] + after(branches[b], behind)
            low_rows = rms_forward(residuals[b], norm2_gain).astype(LOW)
            ffn_full[b] = team_gather(low_rows)
            return low_rows

        def leave(b, behind):
            dffn = after(partial_in[b], behind)
            back, part = rms_backward(residuals[b], norm2_gain, dffn)
            gain2.append(part)
            dresiduals[b] = cot_rows[b].astype(F32) + back
            low_rows = dresiduals[b].astype(LOW)
            dbranch[b] = gather(low_rows)
            return low_rows

        def over_dp(matrix):
            return lax.psum_scatter(matrix, "dp", scatter_dimension=0, tiled=True)

        def joined(halves):
            return jnp.concatenate([jnp.concatenate(h, axis=1) for h in halves], axis=0)

        enter(0, last)
        behind = None
        for b in batches:
            rows = after(ffn_full[b], behind) if b > 0 else ffn_full[b]
            near_half = ffn_half(rows, cot_full[b], near_weights)
            if b + 1 < batch_count:
                behind = enter(b + 1, near_half)
            else:
                behind = leave(b - 1, near_half)
            far_half = ffn_half(after(ffn_full[b], behind), cot_full[b], far_weights)
            hiddens[b] = [near_half[0], far_half[0]]
            dboths[b] = [near_half[1], far_half[1]]
            if b == batch_count - 1:
                down_local = contract_rows(
                    after(jnp.concatenate(cot_full, axis=0), far_half), joined(hiddens)
                ).astype(LOW)
                near_half, far_half = after((near_half, far_half), down_local)
            dffn = contract_cols(near_half[1], ffn_both) + contract_cols(
                far_half[1], far_weights[0]
            )
            partial_in[b] = team_scatter(dffn)
            ffn_out = dot(near_half[0], ffn_down) + dot(far_half[0], far_weights[1])
            partial_out[b] = team_scatter(ffn_out)
            behind = (dffn.astype(LOW), ffn_out.astype(LOW))
        outputs = [(residuals[b] + partial_out[b]).astype(LOW) for b in batches]

        both_local = contract_rows(
            after(jnp.concatenate(ffn_full, axis=0), behind), joined(dboths)
        ).astype(LOW)
        leave(batch_count - 1, both_local)
        down_grad = over_dp(down_local)
        both_grad = over_dp(both_local)
        far_grads = [
            lax.ppermute(down_grad[:, ffn_cols:], "tensor", across),
            lax.ppermute(both_grad[:, 2 * ffn_cols :], "tensor", across),
        ]
        down_grad = spread(down_grad[:, :ffn_cols] + far_grads[0])
        both_grad = spread(both_grad[:, : 2 * ffn_cols] + far_grads[1])

        input_grads, gain1, dtaps, dsmall, dgain = [], [], [], [], []
        grads_out, grads_proj = [], []
        behind = both_local
        for b in batches:
            rows = after(dbranch[b], behind)
            dmixed = contract_cols(rows, output_weight)
            dproj, dt, ds, dg = mixer_backward(
                projs[b], aux[b], taps, params, gain, saveds[b], dmixed, heads
            )
            dtaps.append(dt)
            dsmall.append(ds)
            dgain.append(dg)
            if b == 0:
                pass
            else:
                dproj = after(dproj, dnormed)
            dnormed_low = contract_cols(dproj, proj_all).astype(LOW)
            behind = dnormed_low
            dnormed = scatter_direct(dnormed_low)
            back, part = rms_backward(x_rows[b], norm1_gain, dnormed)
            gain1.append(part)
            input_grads.append((dresiduals[b] + back).astype(LOW))
            grads_proj.append((normed[b], dproj))
            grads_out.append((mixeds[b], rows))
        total_out = sum(contract_rows(after(left, behind), right) for left, right in grads_out)
        total_proj = sum(contract_rows(after(left, behind), right) for left, right in grads_proj)
        total_proj = after(total_proj.astype(LOW), dnormed)
        sum_out, sum_proj = lax.psum((total_out.astype(LOW), total_proj), "dp")
        sum_taps = sum(dtaps).reshape(4, 8, -1).sum(axis=1)
        sum_small = sum(dsmall).reshape(2, 8, LANES).sum(axis=1)[:, :heads]
        sum_taps, sum_small = lax.psum((sum_taps, sum_small), "dp")
        gains = lax.psum((sum(gain1), sum(gain2), sum(dgain).sum(axis=0)), ("dp", "tensor"))
        grad_proj = sum_proj.astype(F32)
        grad_ffn = both_grad.astype(F32)
        small_at = 2 * qk_cols + 2 * v_cols
        return (
            jnp.stack(outputs, axis=0),
            jnp.stack(input_grads, axis=0),
            gains[0],
            grad_proj[:, :qk_cols],
            grad_proj[:, qk_cols : 2 * qk_cols],
            grad_proj[:, 2 * qk_cols : 2 * qk_cols + v_cols],
            grad_proj[:, 2 * qk_cols + v_cols : small_at],
            grad_proj[:, small_at : small_at + 2 * heads].reshape(width, 2, heads),
            sum_taps[:, :qk_cols],
            sum_taps[:, qk_cols : 2 * qk_cols],
            sum_taps[:, 2 * qk_cols :],
            sum_small[0],
            sum_small[1],
            gains[2],
            sum_out.astype(F32),
            gains[1],
            grad_ffn[:, :ffn_cols],
            grad_ffn[:, ffn_cols:],
            jnp.transpose(down_grad).astype(F32),
        )

    return body


def solution(mesh):
    in_specs = (
        P(None, ("dp", "tensor"), None),
        P(None, "dp"),
        P(None, ("dp", "tensor"), None),
        P(),
        P(None, "tensor"),
        P(None, "tensor"),
        P(None, "tensor"),
        P(None, "tensor"),
        P(None, None, "tensor"),
        P(None, "tensor"),
        P(None, "tensor"),
        P(None, "tensor"),
        P("tensor"),
        P("tensor"),
        P(),
        P("tensor", None),
        P(),
        P(None, "tensor"),
        P(None, "tensor"),
        P("tensor", None),
    )
    out_specs = (
        P(None, ("dp", "tensor"), None),
        P(None, ("dp", "tensor"), None),
        P(),
        P(None, "tensor"),
        P(None, "tensor"),
        P(None, "tensor"),
        P(None, "tensor"),
        P(None, None, "tensor"),
        P(None, "tensor"),
        P(None, "tensor"),
        P(None, "tensor"),
        P("tensor"),
        P("tensor"),
        P(),
        P("tensor", None),
        P(),
        P(None, "tensor"),
        P(None, "tensor"),
        P("tensor", None),
    )
    body = make_body(mesh.shape["tensor"], mesh.shape["dp"])
    return jax.shard_map(
        body, mesh=mesh, in_specs=in_specs, out_specs=out_specs, check_vma=False
    )
```

```python
import functools
import jax
import jax.numpy as jnp
from jax import lax
from jax.experimental import pallas as pl
from jax.experimental.pallas import tpu as pltpu
from jax.sharding import PartitionSpec as P

SPAN = 64
LANES = 128
HALO = 8
DK = 128
DV = 256
LOW = jnp.bfloat16
F32 = jnp.float32


def mm(left, right):
    return jnp.dot(left.astype(LOW), right.astype(LOW), preferred_element_type=F32)


def mm_tb(left, right):
    return lax.dot_general(
        left.astype(LOW), right.astype(LOW), (((1,), (1,)), ((), ())), preferred_element_type=F32
    )


def mm_ta(left, right):
    return lax.dot_general(
        left.astype(LOW), right.astype(LOW), (((0,), (0,)), ((), ())), preferred_element_type=F32
    )


def mm_exact(left, right):
    return jnp.dot(left, right, precision=lax.Precision.HIGHEST, preferred_element_type=F32)


def grid_pair(rows, cols):
    return (
        lax.broadcasted_iota(jnp.int32, (rows, cols), 0),
        lax.broadcasted_iota(jnp.int32, (rows, cols), 1),
    )


def lower_inverses(strict_lowers):
    row, col = grid_pair(SPAN, SPAN)
    eye = (row == col).astype(F32)
    size = 1
    inverses = None
    while size < SPAN:
        fresh = (row // (2 * size) == col // (2 * size)) & (row // size != col // size)
        parts = [jnp.where(fresh, lower, 0.0) for lower in strict_lowers]
        if size == 1:
            inverses = [eye - part for part in parts]
        else:
            lows = [inverse.astype(LOW) for inverse in inverses]
            firsts = [mm(part, low) for part, low in zip(parts, lows)]
            inverses = [
                inverse - mm(low, first) for inverse, low, first in zip(inverses, lows, firsts)
            ]
        size *= 2
    return inverses


def gates(small, params):
    rate = small + params[1:2, :]
    soft = jnp.maximum(rate, 0.0) + jnp.log1p(jnp.exp(-jnp.abs(rate)))
    return rate, params[0:1, :] * soft, jax.nn.sigmoid(small)


def decay_tables(decay, aux):
    row, col = grid_pair(SPAN, SPAN)
    running = mm_exact((row >= col).astype(F32), decay)
    lane = lax.broadcasted_iota(jnp.int32, (SPAN, LANES), 1)
    flipped = jnp.transpose(jnp.where(lane == LANES - 1, aux[:, 0:1], running))
    growth = jnp.exp(running) * aux[:, 1:2]
    tail = jnp.exp(jnp.where(aux[:, 2:3] > 0.0, running[SPAN - 1 : SPAN, :] - running, -1e30))
    keep = (aux[:, 0:1] == flipped[LANES - 1 : LANES, :]) & (row >= col)
    return running, flipped, growth, tail, keep


def conv_in(window_ref, start, width, taps, aux):
    total = taps[0:1, start : start + width] * window_ref[HALO : HALO + SPAN, start : start + width]
    for offset in range(1, 4):
        shifted = window_ref[HALO - offset : HALO - offset + SPAN, start : start + width]
        total = total + taps[offset : offset + 1, start : start + width] * (
            shifted * aux[:, 2 + offset : 3 + offset]
        )
    return total


def unit(values):
    return values * lax.rsqrt(jnp.sum(values * values, axis=-1, keepdims=True) + 1e-06)


def forward_kernel(
    heads, proj_ref, halo_ref, aux_ref, taps_ref, params_ref, gain_ref,
    mixed_ref, delta_ref, solved_ref, inverse_ref, entry_ref, memory_ref, window_ref,
):
    qk_cols, v_cols = heads * DK, heads * DV
    gate_at = 2 * qk_cols + v_cols
    small_at = gate_at + v_cols

    @pl.when(pl.program_id(0) == 0)
    def _():
        memory_ref[...] = jnp.zeros_like(memory_ref)

    window_ref[0:HALO, :] = halo_ref[:, 0:gate_at]
    window_ref[HALO : HALO + SPAN, :] = proj_ref[:, 0:gate_at]
    aux = aux_ref[...]
    taps = taps_ref[...]
    _, decay, writes = gates(proj_ref[:, small_at : small_at + LANES], params_ref[...])
    running, flipped, growth, tail, keep = decay_tables(decay, aux)
    row, col = grid_pair(SPAN, SPAN)
    each = range(heads)
    queries = [
        unit(jax.nn.silu(conv_in(window_ref, h * DK, DK, taps, aux))) * DK ** (-0.5) for h in each
    ]
    keys = [
        unit(jax.nn.silu(conv_in(window_ref, qk_cols + h * DK, DK, taps, aux))) for h in each
    ]
    boths = [
        jnp.concatenate([query.astype(LOW), key.astype(LOW)], axis=0)
        for query, key in zip(queries, keys)
    ]
    scores = [mm_tb(both, both[SPAN:]) for both in boths]
    withins = [
        jnp.exp(jnp.where(keep, running[:, h : h + 1] - flipped[h : h + 1, :], -1e30))
        for h in each
    ]
    betas = [writes[:, heads + h : heads + h + 1] for h in each]
    grows = [growth[:, h : h + 1] for h in each]
    inverses = lower_inverses(
        [
            betas[h] * scores[h][SPAN:] * jnp.where(row > col, withins[h], 0.0)
            for h in each
        ]
    )
    inverses = [inverse.astype(LOW) for inverse in inverses]
    memories = [memory_ref[h] for h in each]
    lows = [memory.astype(LOW) for memory in memories]
    reads = [mm(both, low) for both, low in zip(boths, lows)]
    values = [
        jax.nn.silu(conv_in(window_ref, 2 * qk_cols + h * DV, DV, taps, aux)) for h in each
    ]
    targets = [betas[h] * (values[h] - grows[h] * reads[h][SPAN:]) for h in each]
    solveds = [mm(inverses[h], targets[h]).astype(LOW) for h in each]
    updates = [mm_ta(tail[:, h : h + 1] * keys[h], solveds[h]) for h in each]
    deltas = [
        grows[h] * reads[h][:SPAN] + mm(scores[h][:SPAN] * withins[h], solveds[h]) for h in each
    ]
    for h in each:
        entry_ref[0, h] = lows[h]
        inverse_ref[0, h] = inverses[h]
        memory_ref[h] = grows[h][SPAN - 1 : SPAN, :] * memories[h] + updates[h]
        cols = slice(h * DV, (h + 1) * DV)
        delta = deltas[h]
        solved_ref[:, cols] = solveds[h]
        delta_ref[:, cols] = delta
        scaled = delta * lax.rsqrt(jnp.mean(delta * delta, axis=-1, keepdims=True) + 1e-05)
        gate = proj_ref[:, gate_at + h * DV : gate_at + (h + 1) * DV]
        mixed_ref[:, cols] = (scaled * gain_ref[0:1, :] * jax.nn.silu(gate)).astype(LOW)


def silu_back(values, grad):
    sig = jax.nn.sigmoid(values)
    return grad * sig * (1.0 + values * (1.0 - sig))


def fold(values):
    total = values[0:8]
    for part in range(1, values.shape[0] // 8):
        total = total + values[8 * part : 8 * part + 8]
    return total


def backward_kernel(
    heads, proj_ref, halo_ref, aux_ref, taps_ref, params_ref, gain_ref,
    delta_ref, solved_ref, inverse_ref, entry_ref, grad_ref,
    dproj_ref, dtaps_ref, dsmall_ref, dgain_ref, dmemory_ref, window_ref, later_ref,
):
    qk_cols, v_cols = heads * DK, heads * DV
    gate_at = 2 * qk_cols + v_cols
    small_at = gate_at + v_cols

    @pl.when(pl.program_id(0) == 0)
    def _():
        dmemory_ref[...] = jnp.zeros_like(dmemory_ref)
        later_ref[...] = jnp.zeros_like(later_ref)
        dtaps_ref[...] = jnp.zeros_like(dtaps_ref)
        dsmall_ref[...] = jnp.zeros_like(dsmall_ref)
        dgain_ref[...] = jnp.zeros_like(dgain_ref)

    window_ref[0:HALO, :] = halo_ref[:, 0:gate_at]
    window_ref[HALO : HALO + SPAN, :] = proj_ref[:, 0:gate_at]
    later_ref[SPAN : SPAN + HALO, :] = later_ref[0:HALO, :]
    aux = aux_ref[...]
    taps = taps_ref[...]
    small = proj_ref[:, small_at : small_at + LANES]
    rate, decay, writes = gates(small, params_ref[...])
    running, flipped, growth, tail, keep = decay_tables(decay, aux)
    row, col = grid_pair(SPAN, SPAN)
    lane = lax.broadcasted_iota(jnp.int32, (SPAN, LANES), 1)
    upper = (row <= col).astype(F32)
    behind = (row > col).astype(F32)
    dbeta_all = jnp.zeros((SPAN, LANES), F32)
    arrive_all = jnp.zeros((SPAN, LANES), F32)
    leave_all = jnp.zeros((SPAN, LANES), F32)
    direct_all = jnp.zeros((SPAN, LANES), F32)

    def conv_back(pre, grad, start, width):
        dpre = silu_back(pre, grad)
        later_ref[0:SPAN, start : start + width] = dpre
        total = taps[0:1, start : start + width] * dpre
        base = window_ref[HALO : HALO + SPAN, start : start + width]
        dtaps_ref[0:8, start : start + width] += fold(dpre * base)
        for offset in range(1, 4):
            ahead = later_ref[offset : offset + SPAN, start : start + width]
            total = total + taps[offset : offset + 1, start : start + width] * (
                ahead * aux[:, 5 + offset : 6 + offset]
            )
            shifted = window_ref[HALO - offset : HALO - offset + SPAN, start : start + width]
            dtaps_ref[8 * offset : 8 * offset + 8, start : start + width] += fold(
                dpre * (shifted * aux[:, 2 + offset : 3 + offset])
            )
        dproj_ref[:, start : start + width] = total.astype(LOW)

    each = range(heads)
    values_at = [slice(h * DV, (h + 1) * DV) for h in each]
    ddeltas = []
    for h in each:
        delta = delta_ref[:, values_at[h]]
        scale = lax.rsqrt(jnp.mean(delta * delta, axis=-1, keepdims=True) + 1e-05)
        scaled = delta * scale
        gate = proj_ref[:, gate_at + h * DV : gate_at + (h + 1) * DV]
        gsig = jax.nn.sigmoid(gate)
        dmixed = grad_ref[:, values_at[h]]
        gain = gain_ref[0:1, :]
        dproj_ref[:, gate_at + h * DV : gate_at + (h + 1) * DV] = (
            dmixed * scaled * gain * gsig * (1.0 + gate * (1.0 - gsig))
        ).astype(LOW)
        dnormed = dmixed * (gate * gsig)
        dgain_ref[...] += fold(dnormed * scaled)
        dnormed = dnormed * gain
        ddelta = scale * (
            dnormed - scaled * jnp.mean(scaled * dnormed, axis=-1, keepdims=True)
        )
        ddeltas.append(ddelta.astype(LOW))
    q_pres = [conv_in(window_ref, h * DK, DK, taps, aux) for h in each]
    k_pres = [conv_in(window_ref, qk_cols + h * DK, DK, taps, aux) for h in each]
    q_acts = [jax.nn.silu(pre) for pre in q_pres]
    k_acts = [jax.nn.silu(pre) for pre in k_pres]
    q_scales = [
        lax.rsqrt(jnp.sum(act * act, axis=-1, keepdims=True) + 1e-06) for act in q_acts
    ]
    k_scales = [
        lax.rsqrt(jnp.sum(act * act, axis=-1, keepdims=True) + 1e-06) for act in k_acts
    ]
    q_units = [act * scale for act, scale in zip(q_acts, q_scales)]
    keys = [act * scale for act, scale in zip(k_acts, k_scales)]
    queries = [unit_row * DK ** (-0.5) for unit_row in q_units]
    betas = [writes[:, heads + h : heads + h + 1] for h in each]
    grows = [growth[:, h : h + 1] for h in each]
    fades = [tail[:, h : h + 1] for h in each]
    withins = [
        jnp.exp(jnp.where(keep, running[:, h : h + 1] - flipped[h : h + 1, :], -1e30))
        for h in each
    ]
    key_lows = [key.astype(LOW) for key in keys]
    boths = [
        jnp.concatenate([query.astype(LOW), low], axis=0) for query, low in zip(queries, key_lows)
    ]
    scores = [mm_tb(both, low) for both, low in zip(boths, key_lows)]
    solveds = [solved_ref[:, values_at[h]] for h in each]
    entries = [entry_ref[0, h] for h in each]
    dmemories = [dmemory_ref[h] for h in each]
    dmemory_lows = [dmemory.astype(LOW) for dmemory in dmemories]
    leaving = [mm(low, dlow) for low, dlow in zip(key_lows, dmemory_lows)]
    dsolveds = [
        mm_ta(scores[h][:SPAN] * withins[h], ddeltas[h]) + fades[h] * leaving[h] for h in each
    ]
    dtargets = [mm_ta(inverse_ref[0, h], dsolveds[h]) for h in each]
    pairs = [
        jnp.concatenate([ddeltas[h], dtargets[h].astype(LOW)], axis=0) for h in each
    ]
    factors = [
        jnp.concatenate(
            [
                (grows[h] * queries[h]).astype(LOW),
                (-(betas[h] * grows[h]) * keys[h]).astype(LOW),
            ],
            axis=0,
        )
        for h in each
    ]
    flows = [mm_ta(factor, pair) for factor, pair in zip(factors, pairs)]
    carries = []
    for h in each:
        last = grows[h][SPAN - 1 : SPAN, :]
        carries.append(
            last * jnp.sum(dmemories[h] * entries[h].astype(F32), keepdims=True)
        )
        dmemory_ref[h] = last * dmemories[h] + flows[h]
    on_solveds = [mm_tb(pair, solved) for pair, solved in zip(pairs, solveds)]
    on_entries = [mm_tb(pair, entry) for pair, entry in zip(pairs, entries)]
    dkey_leaves = [
        fades[h] * mm_tb(solveds[h], dmemory_lows[h]) for h in each
    ]
    dscores = [on_solveds[h][:SPAN] * withins[h] for h in each]
    dsystems = [
        -on_solveds[h][SPAN:] * jnp.where(row > col, withins[h], 0.0) for h in each
    ]
    dsystem_betas = [betas[h] * dsystems[h] for h in each]
    duos = [
        jnp.concatenate([dscores[h].astype(LOW), dsystem_betas[h].astype(LOW)], axis=0)
        for h in each
    ]
    forths = [mm(duo, low) for duo, low in zip(duos, key_lows)]
    backs = [mm_ta(duo, both) for duo, both in zip(duos, boths)]
    spreads = [
        mm(upper, dscores[h] * scores[h][:SPAN] + dsystem_betas[h] * scores[h][SPAN:])
        for h in each
    ]
    for h in each:
        q_at, k_at, v_at = h * DK, qk_cols + h * DK, 2 * qk_cols + h * DV
        key, query, beta = keys[h], queries[h], betas[h]
        dquery_far = grows[h] * on_entries[h][:SPAN]
        dkey_far = grows[h] * on_entries[h][SPAN:]
        dquery = dquery_far + forths[h][:SPAN]
        dkey = forths[h][SPAN:] + backs[h] - beta * dkey_far + dkey_leaves[h]
        v_pre = conv_in(window_ref, v_at, DV, taps, aux)
        value = jax.nn.silu(v_pre)
        key_far = jnp.sum(key * dkey_far, axis=-1, keepdims=True)
        dbeta = (
            jnp.sum(dtargets[h] * value, axis=-1, keepdims=True)
            - key_far
            + jnp.sum(dsystems[h] * scores[h][SPAN:], axis=-1, keepdims=True)
        )
        arrive = jnp.sum(query * dquery_far, axis=-1, keepdims=True) - beta * key_far
        leave = jnp.sum(key * dkey_leaves[h], axis=-1, keepdims=True)
        direct = jnp.sum(spreads[h] * behind, axis=-1, keepdims=True) + carries[h]
        dbeta_all = jnp.where(lane == heads + h, dbeta, dbeta_all)
        arrive_all = jnp.where(lane == h, arrive, arrive_all)
        leave_all = jnp.where(lane == h, leave, leave_all)
        direct_all = jnp.where(lane == h, direct, direct_all)
        dq_unit = dquery * DK ** (-0.5)
        dq_act = q_scales[h] * (
            dq_unit - q_units[h] * jnp.sum(q_units[h] * dq_unit, axis=-1, keepdims=True)
        )
        dk_act = k_scales[h] * (dkey - key * jnp.sum(key * dkey, axis=-1, keepdims=True))
        conv_back(q_pres[h], dq_act, q_at, DK)
        conv_back(k_pres[h], dk_act, k_at, DK)
        conv_back(v_pre, beta * dtargets[h], v_at, DV)

    ddecay = direct_all + mm_exact(upper, arrive_all) + mm_exact(behind, leave_all)
    drate = ddecay * params_ref[0:1, :] * jax.nn.sigmoid(rate)
    dsmall_ref[0:8, :] += fold(ddecay * decay)
    dsmall_ref[8:16, :] += fold(drate)
    dproj_ref[:, small_at : small_at + LANES] = (
        drate + dbeta_all * writes * (1.0 - writes)
    ).astype(LOW)


def whole(shape):
    return pl.BlockSpec(shape, lambda step: (0,) * len(shape))


def mixer_forward(projected, aux, taps, params, gain, heads):
    rows, width = projected.shape
    v_cols = heads * DV
    conv_cols = taps.shape[1]
    blocks = rows // SPAN
    tall = SPAN // HALO
    return pl.pallas_call(
        functools.partial(forward_kernel, heads),
        grid=(blocks,),
        in_specs=[
            pl.BlockSpec((SPAN, width), lambda c: (c, 0)),
            pl.BlockSpec((HALO, width), lambda c: (jnp.maximum(c * tall - 1, 0), 0)),
            pl.BlockSpec((SPAN, LANES), lambda c: (c, 0)),
            whole(taps.shape),
            whole(params.shape),
            whole((8, DV)),
        ],
        out_specs=[
            pl.BlockSpec((SPAN, v_cols), lambda c: (c, 0)),
            pl.BlockSpec((SPAN, v_cols), lambda c: (c, 0)),
            pl.BlockSpec((SPAN, v_cols), lambda c: (c, 0)),
            pl.BlockSpec((1, heads, SPAN, SPAN), lambda c: (c, 0, 0, 0)),
            pl.BlockSpec((1, heads, DK, DV), lambda c: (c, 0, 0, 0)),
        ],
        out_shape=[
            jax.ShapeDtypeStruct((rows, v_cols), LOW),
            jax.ShapeDtypeStruct((rows, v_cols), F32),
            jax.ShapeDtypeStruct((rows, v_cols), LOW),
            jax.ShapeDtypeStruct((blocks, heads, SPAN, SPAN), LOW),
            jax.ShapeDtypeStruct((blocks, heads, DK, DV), LOW),
        ],
        scratch_shapes=[
            pltpu.VMEM((heads, DK, DV), F32),
            pltpu.VMEM((SPAN + HALO, conv_cols), F32),
        ],
        compiler_params=pltpu.CompilerParams(vmem_limit_bytes=40 << 20),
        cost_estimate=pl.CostEstimate(
            flops=rows, bytes_accessed=rows, transcendentals=0
        ),
        name="mixer_forward",
    )(projected, projected, aux, taps, params, gain)


def mixer_backward(projected, aux, taps, params, gain, saved, grad, heads):
    delta, solved, inverse, entry = saved
    rows, width = projected.shape
    v_cols = heads * DV
    conv_cols = taps.shape[1]
    blocks = rows // SPAN
    tall = SPAN // HALO
    last = blocks - 1
    return pl.pallas_call(
        functools.partial(backward_kernel, heads),
        grid=(blocks,),
        in_specs=[
            pl.BlockSpec((SPAN, width), lambda c: (last - c, 0)),
            pl.BlockSpec((HALO, width), lambda c: (jnp.maximum((last - c) * tall - 1, 0), 0)),
            pl.BlockSpec((SPAN, LANES), lambda c: (last - c, 0)),
            whole(taps.shape),
            whole(params.shape),
            whole((8, DV)),
            pl.BlockSpec((SPAN, v_cols), lambda c: (last - c, 0)),
            pl.BlockSpec((SPAN, v_cols), lambda c: (last - c, 0)),
            pl.BlockSpec((1, heads, SPAN, SPAN), lambda c: (last - c, 0, 0, 0)),
            pl.BlockSpec((1, heads, DK, DV), lambda c: (last - c, 0, 0, 0)),
            pl.BlockSpec((SPAN, v_cols), lambda c: (last - c, 0)),
        ],
        out_specs=[
            pl.BlockSpec((SPAN, width), lambda c: (last - c, 0)),
            whole((32, conv_cols)),
            whole((16, LANES)),
            whole((8, DV)),
        ],
        out_shape=[
            jax.ShapeDtypeStruct((rows, width), LOW),
            jax.ShapeDtypeStruct((32, conv_cols), F32),
            jax.ShapeDtypeStruct((16, LANES), F32),
            jax.ShapeDtypeStruct((8, DV), F32),
        ],
        scratch_shapes=[
            pltpu.VMEM((heads, DK, DV), F32),
            pltpu.VMEM((SPAN + HALO, conv_cols), F32),
            pltpu.VMEM((SPAN + HALO, conv_cols), F32),
        ],
        compiler_params=pltpu.CompilerParams(vmem_limit_bytes=48 << 20),
        cost_estimate=pl.CostEstimate(
            flops=rows, bytes_accessed=rows, transcendentals=0
        ),
        name="mixer_backward",
    )(projected, projected, aux, taps, params, gain, delta, solved, inverse, entry, grad)


def token_tables(segments):
    rows = segments.shape[0]
    seg = segments.astype(F32)
    blocked = seg.reshape(rows // SPAN, SPAN)
    ends = blocked[:, SPAN - 1]
    before = jnp.concatenate([jnp.full((1,), -1.0, F32), ends[:-1]])
    columns = [
        seg,
        (blocked == before[:, None]).astype(F32).reshape(rows),
        (blocked == ends[:, None]).astype(F32).reshape(rows),
    ]
    links = [(seg[offset:] == seg[:-offset]).astype(F32) for offset in range(1, 4)]
    columns += [jnp.pad(link, (offset, 0)) for offset, link in enumerate(links, 1)]
    columns += [jnp.pad(link, (0, offset)) for offset, link in enumerate(links, 1)]
    return jnp.pad(jnp.stack(columns, axis=1), ((0, 0), (0, LANES - len(columns))))


def rms_forward(values, gain_vec):
    scale = lax.rsqrt(jnp.mean(values * values, axis=-1, keepdims=True) + 1e-05)
    return values * scale * gain_vec


def rms_backward(values, gain_vec, grad):
    scale = lax.rsqrt(jnp.mean(values * values, axis=-1, keepdims=True) + 1e-05)
    scaled = values * scale
    inner = grad * gain_vec
    back = scale * (inner - scaled * jnp.mean(scaled * inner, axis=-1, keepdims=True))
    return back, jnp.sum(grad * scaled, axis=0)


def dot(left, right):
    return jnp.dot(left, right, preferred_element_type=F32)


def contract_rows(left, right):
    return lax.dot_general(
        left, right, (((0,), (0,)), ((), ())), preferred_element_type=F32
    )


def contract_cols(left, right):
    return lax.dot_general(
        left, right, (((1,), (1,)), ((), ())), preferred_element_type=F32
    )


def gather(rows):
    return lax.all_gather(rows, "tensor", axis=0, tiled=True)


def scatter(rows):
    return lax.psum_scatter(
        rows.astype(LOW), "tensor", scatter_dimension=0, tiled=True
    ).astype(F32)


def after(values, first):
    return lax.optimization_barrier((values, first))[0]


def make_body(parts, replicas):
    near = parts // 2
    teams = [list(range(near)), list(range(near, parts))]
    swap = [(i, i ^ 1) for i in range(parts)]
    across = [(i, (i + near) % parts) for i in range(parts)]

    def team_exchange(rows):
        if near == 2:
            return lax.ppermute(rows, "tensor", swap)
        return lax.all_gather(rows, "tensor", axis=0, tiled=True, axis_index_groups=teams)

    def team_join(rows, others):
        return jnp.concatenate([rows, others], axis=0) if near == 2 else others

    def team_gather(rows):
        return team_join(rows, team_exchange(rows))

    def team_scatter(rows):
        if near == 2:
            half = rows.shape[0] // 2
            return rows[:half] + lax.ppermute(rows[half:].astype(LOW), "tensor", swap).astype(F32)
        return lax.psum_scatter(
            rows.astype(LOW), "tensor", scatter_dimension=0, tiled=True, axis_index_groups=teams
        ).astype(F32)

    def scatter_direct(rows):
        size = rows.shape[0] // parts
        place = lax.axis_index("tensor")

        def part(hop):
            index = lax.rem(place + hop, parts)
            return lax.dynamic_slice_in_dim(rows, index * size, size)

        total = part(0).astype(F32)
        for hop in range(1, parts):
            pairs = [(i, (i + hop) % parts) for i in range(parts)]
            total = total + lax.ppermute(part(hop).astype(LOW), "tensor", pairs).astype(F32)
        return total

    def own_piece(matrix):
        rows = matrix.shape[0] // replicas
        return lax.dynamic_slice_in_dim(matrix, lax.axis_index("dp") * rows, rows)

    def spread(piece):
        return lax.all_gather(piece, "dp", axis=0, tiled=True)

    def body(
        block_input,
        segment_ids,
        out_cotangent,
        norm1_gain,
        query_weight,
        key_weight,
        value_weight,
        gate_weight,
        decay_weight,
        conv_query,
        conv_key,
        conv_value,
        decay_log,
        decay_bias,
        output_gain,
        output_weight,
        norm2_gain,
        ffn_gate,
        ffn_up,
        ffn_down,
    ):
        batch_count, slice_rows, width = block_input.shape
        heads = decay_log.shape[0]
        qk_cols = query_weight.shape[1]
        v_cols = value_weight.shape[1]
        ffn_cols = ffn_gate.shape[1]
        batches = range(batch_count)
        x_rows = [block_input[b].astype(F32) for b in batches]
        cot_rows = [out_cotangent[b] for b in batches]
        first_rows = [rms_forward(x_rows[b], norm1_gain).astype(LOW) for b in batches]
        ffn_both = jnp.concatenate([ffn_gate, ffn_up], axis=1)
        proj_all = jnp.concatenate(
            [
                query_weight,
                key_weight,
                value_weight,
                gate_weight,
                decay_weight.reshape(width, 2 * heads),
                jnp.zeros((width, LANES - 2 * heads), LOW),
            ],
            axis=1,
        )
        taps = jnp.pad(
            jnp.concatenate([conv_query, conv_key, conv_value], axis=1), ((0, 4), (0, 0))
        )
        params = jnp.pad(
            jnp.stack([-jnp.exp(decay_log), decay_bias]), ((0, 6), (0, LANES - heads))
        )
        gain = jnp.broadcast_to(output_gain, (8, output_gain.shape[0]))
        aux = [token_tables(segment_ids[b]) for b in batches]

        normed, projs, mixeds, saveds, branches, cot_full = [], [], [], [], [], []
        pieces = [own_piece(ffn_both), own_piece(ffn_down)]
        far = None
        for b in batches:
            rows = first_rows[b]
            if b > 0:
                rows = after(rows, normed[b - 1])
            normed.append(gather(rows))
        pieces = [
            lax.ppermute(after(piece, proj_all), "tensor", across) for piece in pieces
        ]
        far = [spread(piece) for piece in pieces]
        cot_pairs = [team_exchange(after(rows, pieces)) for rows in cot_rows]
        cot_full = [team_join(cot_rows[b], cot_pairs[b]) for b in batches]
        for b in batches:
            rows = after(normed[b], branches[b - 1]) if b > 0 else normed[b]
            projected = dot(rows, proj_all)
            mixed, *saved = mixer_forward(projected, aux[b], taps, params, gain, heads)
            mixed = after(mixed, pieces if b == 0 else cot_pairs)
            projs.append(projected)
            mixeds.append(mixed)
            saveds.append(saved)
            branches.append(dot(mixed, output_weight).astype(LOW))
        last = branches[-1]
        branches = [scatter(rows) for rows in branches]

        near_weights, far_weights = (ffn_both, ffn_down), tuple(far)

        def ffn_half(rows, cot, weights):
            both, down = weights
            gate_up = dot(rows, both)
            gate_pre, up_pre = gate_up[:, :ffn_cols], gate_up[:, ffn_cols:]
            sig = jax.nn.sigmoid(gate_pre)
            hidden = (gate_pre * sig * up_pre).astype(LOW)
            dhidden = contract_cols(cot, down)
            dgate = dhidden * up_pre * sig * (1.0 + gate_pre * (1.0 - sig))
            dup = dhidden * (gate_pre * sig)
            return hidden, jnp.concatenate([dgate, dup], axis=1).astype(LOW)

        residuals = [None] * batch_count
        ffn_full = [None] * batch_count
        hiddens = [None] * batch_count
        dboths = [None] * batch_count
        partial_in = [None] * batch_count
        partial_out = [None] * batch_count
        dresiduals = [None] * batch_count
        dbranch = [None] * batch_count
        gain2 = []

        def enter(b, behind):
            residuals[b] = x_rows[b] + after(branches[b], behind)
            low_rows = rms_forward(residuals[b], norm2_gain).astype(LOW)
            ffn_full[b] = team_gather(low_rows)
            return low_rows

        def leave(b, behind):
            dffn = after(partial_in[b], behind)
            back, part = rms_backward(residuals[b], norm2_gain, dffn)
            gain2.append(part)
            dresiduals[b] = cot_rows[b].astype(F32) + back
            low_rows = dresiduals[b].astype(LOW)
            dbranch[b] = gather(low_rows)
            return low_rows

        def over_dp(matrix):
            return lax.psum_scatter(matrix, "dp", scatter_dimension=0, tiled=True)

        def joined(halves):
            return jnp.concatenate([jnp.concatenate(h, axis=1) for h in halves], axis=0)

        enter(0, last)
        behind = None
        for b in batches:
            rows = after(ffn_full[b], behind) if b > 0 else ffn_full[b]
            near_half = ffn_half(rows, cot_full[b], near_weights)
            if b + 1 < batch_count:
                behind = enter(b + 1, near_half)
            else:
                behind = leave(b - 1, near_half)
            far_half = ffn_half(after(ffn_full[b], behind), cot_full[b], far_weights)
            hiddens[b] = [near_half[0], far_half[0]]
            dboths[b] = [near_half[1], far_half[1]]
            if b == batch_count - 1:
                down_local = contract_rows(
                    after(jnp.concatenate(cot_full, axis=0), far_half), joined(hiddens)
                ).astype(LOW)
                near_half, far_half = after((near_half, far_half), down_local)
            dffn = contract_cols(near_half[1], ffn_both) + contract_cols(
                far_half[1], far_weights[0]
            )
            partial_in[b] = team_scatter(dffn)
            ffn_out = dot(near_half[0], ffn_down) + dot(far_half[0], far_weights[1])
            partial_out[b] = team_scatter(ffn_out)
            behind = (dffn.astype(LOW), ffn_out.astype(LOW))
        outputs = [(residuals[b] + partial_out[b]).astype(LOW) for b in batches]

        both_local = contract_rows(
            after(jnp.concatenate(ffn_full, axis=0), behind), joined(dboths)
        ).astype(LOW)
        leave(batch_count - 1, both_local)
        down_grad = over_dp(down_local)
        both_grad = over_dp(both_local)
        down_other = lax.ppermute(down_grad[:, ffn_cols:], "tensor", across)

        input_grads, gain1, dtaps, dsmall, dgain = [], [], [], [], []
        grads_out, grads_proj = [], []
        behind = both_local
        for b in batches:
            rows = after(dbranch[b], behind)
            dmixed = contract_cols(rows, output_weight)
            dproj, dt, ds, dg = mixer_backward(
                projs[b], aux[b], taps, params, gain, saveds[b], dmixed, heads
            )
            dtaps.append(dt)
            dsmall.append(ds)
            dgain.append(dg)
            dproj = after(dproj, down_other if b == 0 else dnormed)
            dnormed_low = contract_cols(dproj, proj_all).astype(LOW)
            behind = dnormed_low
            dnormed = scatter_direct(dnormed_low)
            back, part = rms_backward(x_rows[b], norm1_gain, dnormed)
            gain1.append(part)
            input_grads.append((dresiduals[b] + back).astype(LOW))
            grads_proj.append((normed[b], dproj))
            grads_out.append((mixeds[b], rows))
        total_out = sum(contract_rows(after(left, behind), right) for left, right in grads_out)
        total_proj = sum(contract_rows(after(left, behind), right) for left, right in grads_proj)
        total_proj = after(total_proj.astype(LOW), dnormed)
        both_other = lax.ppermute(
            both_grad[:, 2 * ffn_cols :], "tensor", across
        )
        down_grad = spread(down_grad[:, :ffn_cols] + down_other)
        both_grad = spread(both_grad[:, : 2 * ffn_cols] + both_other)
        sum_out, sum_proj = lax.psum((total_out.astype(LOW), total_proj), "dp")
        sum_taps = sum(dtaps).reshape(4, 8, -1).sum(axis=1)
        sum_small = sum(dsmall).reshape(2, 8, LANES).sum(axis=1)[:, :heads]
        sum_taps, sum_small = lax.psum((sum_taps, sum_small), "dp")
        gains = lax.psum((sum(gain1), sum(gain2), sum(dgain).sum(axis=0)), ("dp", "tensor"))
        grad_proj = sum_proj.astype(F32)
        grad_ffn = both_grad.astype(F32)
        small_at = 2 * qk_cols + 2 * v_cols
        return (
            jnp.stack(outputs, axis=0),
            jnp.stack(input_grads, axis=0),
            gains[0],
            grad_proj[:, :qk_cols],
            grad_proj[:, qk_cols : 2 * qk_cols],
            grad_proj[:, 2 * qk_cols : 2 * qk_cols + v_cols],
            grad_proj[:, 2 * qk_cols + v_cols : small_at],
            grad_proj[:, small_at : small_at + 2 * heads].reshape(width, 2, heads),
            sum_taps[:, :qk_cols],
            sum_taps[:, qk_cols : 2 * qk_cols],
            sum_taps[:, 2 * qk_cols :],
            sum_small[0],
            sum_small[1],
            gains[2],
            sum_out.astype(F32),
            gains[1],
            grad_ffn[:, :ffn_cols],
            grad_ffn[:, ffn_cols:],
            jnp.transpose(down_grad).astype(F32),
        )

    return body


def solution(mesh):
    in_specs = (
        P(None, ("dp", "tensor"), None),
        P(None, "dp"),
        P(None, ("dp", "tensor"), None),
        P(),
        P(None, "tensor"),
        P(None, "tensor"),
        P(None, "tensor"),
        P(None, "tensor"),
        P(None, None, "tensor"),
        P(None, "tensor"),
        P(None, "tensor"),
        P(None, "tensor"),
        P("tensor"),
        P("tensor"),
        P(),
        P("tensor", None),
        P(),
        P(None, "tensor"),
        P(None, "tensor"),
        P("tensor", None),
    )
    out_specs = (
        P(None, ("dp", "tensor"), None),
        P(None, ("dp", "tensor"), None),
        P(),
        P(None, "tensor"),
        P(None, "tensor"),
        P(None, "tensor"),
        P(None, "tensor"),
        P(None, None, "tensor"),
        P(None, "tensor"),
        P(None, "tensor"),
        P(None, "tensor"),
        P("tensor"),
        P("tensor"),
        P(),
        P("tensor", None),
        P(),
        P(None, "tensor"),
        P(None, "tensor"),
        P("tensor", None),
    )
    body = make_body(mesh.shape["tensor"], mesh.shape["dp"])
    return jax.shard_map(
        body, mesh=mesh, in_specs=in_specs, out_specs=out_specs, check_vma=False
    )
```

```python
import functools
import jax
import jax.numpy as jnp
from jax import lax
from jax.experimental import pallas as pl
from jax.experimental.pallas import tpu as pltpu
from jax.sharding import PartitionSpec as P

SPAN = 64
LANES = 128
HALO = 8
DK = 128
DV = 256
LOW = jnp.bfloat16
F32 = jnp.float32


def mm(left, right):
    return jnp.dot(left.astype(LOW), right.astype(LOW), preferred_element_type=F32)


def mm_tb(left, right):
    return lax.dot_general(
        left.astype(LOW), right.astype(LOW), (((1,), (1,)), ((), ())), preferred_element_type=F32
    )


def mm_ta(left, right):
    return lax.dot_general(
        left.astype(LOW), right.astype(LOW), (((0,), (0,)), ((), ())), preferred_element_type=F32
    )


def mm_exact(left, right):
    return jnp.dot(left, right, precision=lax.Precision.HIGHEST, preferred_element_type=F32)


def grid_pair(rows, cols):
    return (
        lax.broadcasted_iota(jnp.int32, (rows, cols), 0),
        lax.broadcasted_iota(jnp.int32, (rows, cols), 1),
    )


def lower_inverses(strict_lowers):
    row, col = grid_pair(SPAN, SPAN)
    eye = (row == col).astype(F32)
    size = 1
    inverses = None
    while size < SPAN:
        fresh = (row // (2 * size) == col // (2 * size)) & (row // size != col // size)
        parts = [jnp.where(fresh, lower, 0.0) for lower in strict_lowers]
        if size == 1:
            inverses = [eye - part for part in parts]
        else:
            lows = [inverse.astype(LOW) for inverse in inverses]
            firsts = [mm(part, low) for part, low in zip(parts, lows)]
            inverses = [
                inverse - mm(low, first) for inverse, low, first in zip(inverses, lows, firsts)
            ]
        size *= 2
    return inverses


def gates(small, params):
    rate = small + params[1:2, :]
    soft = jnp.maximum(rate, 0.0) + jnp.log1p(jnp.exp(-jnp.abs(rate)))
    return rate, params[0:1, :] * soft, jax.nn.sigmoid(small)


def decay_tables(decay, aux):
    row, col = grid_pair(SPAN, SPAN)
    running = mm_exact((row >= col).astype(F32), decay)
    lane = lax.broadcasted_iota(jnp.int32, (SPAN, LANES), 1)
    flipped = jnp.transpose(jnp.where(lane == LANES - 1, aux[:, 0:1], running))
    growth = jnp.exp(running) * aux[:, 1:2]
    tail = jnp.exp(jnp.where(aux[:, 2:3] > 0.0, running[SPAN - 1 : SPAN, :] - running, -1e30))
    keep = (aux[:, 0:1] == flipped[LANES - 1 : LANES, :]) & (row >= col)
    return running, flipped, growth, tail, keep


def conv_in(window_ref, start, width, taps, aux):
    total = taps[0:1, start : start + width] * window_ref[HALO : HALO + SPAN, start : start + width]
    for offset in range(1, 4):
        shifted = window_ref[HALO - offset : HALO - offset + SPAN, start : start + width]
        total = total + taps[offset : offset + 1, start : start + width] * (
            shifted * aux[:, 2 + offset : 3 + offset]
        )
    return total


def unit(values):
    return values * lax.rsqrt(jnp.sum(values * values, axis=-1, keepdims=True) + 1e-06)


def forward_kernel(
    heads, proj_ref, halo_ref, aux_ref, taps_ref, params_ref, gain_ref,
    mixed_ref, delta_ref, solved_ref, inverse_ref, entry_ref, memory_ref, window_ref,
):
    qk_cols, v_cols = heads * DK, heads * DV
    gate_at = 2 * qk_cols + v_cols
    small_at = gate_at + v_cols

    @pl.when(pl.program_id(0) == 0)
    def _():
        memory_ref[...] = jnp.zeros_like(memory_ref)

    window_ref[0:HALO, :] = halo_ref[:, 0:gate_at]
    window_ref[HALO : HALO + SPAN, :] = proj_ref[:, 0:gate_at]
    aux = aux_ref[...]
    taps = taps_ref[...]
    _, decay, writes = gates(proj_ref[:, small_at : small_at + LANES], params_ref[...])
    running, flipped, growth, tail, keep = decay_tables(decay, aux)
    row, col = grid_pair(SPAN, SPAN)
    each = range(heads)
    queries = [
        unit(jax.nn.silu(conv_in(window_ref, h * DK, DK, taps, aux))) * DK ** (-0.5) for h in each
    ]
    keys = [
        unit(jax.nn.silu(conv_in(window_ref, qk_cols + h * DK, DK, taps, aux))) for h in each
    ]
    boths = [
        jnp.concatenate([query.astype(LOW), key.astype(LOW)], axis=0)
        for query, key in zip(queries, keys)
    ]
    scores = [mm_tb(both, both[SPAN:]) for both in boths]
    withins = [
        jnp.exp(jnp.where(keep, running[:, h : h + 1] - flipped[h : h + 1, :], -1e30))
        for h in each
    ]
    betas = [writes[:, heads + h : heads + h + 1] for h in each]
    grows = [growth[:, h : h + 1] for h in each]
    inverses = lower_inverses(
        [
            betas[h] * scores[h][SPAN:] * jnp.where(row > col, withins[h], 0.0)
            for h in each
        ]
    )
    inverses = [inverse.astype(LOW) for inverse in inverses]
    memories = [memory_ref[h] for h in each]
    lows = [memory.astype(LOW) for memory in memories]
    reads = [mm(both, low) for both, low in zip(boths, lows)]
    values = [
        jax.nn.silu(conv_in(window_ref, 2 * qk_cols + h * DV, DV, taps, aux)) for h in each
    ]
    targets = [betas[h] * (values[h] - grows[h] * reads[h][SPAN:]) for h in each]
    solveds = [mm(inverses[h], targets[h]).astype(LOW) for h in each]
    updates = [mm_ta(tail[:, h : h + 1] * keys[h], solveds[h]) for h in each]
    deltas = [
        grows[h] * reads[h][:SPAN] + mm(scores[h][:SPAN] * withins[h], solveds[h]) for h in each
    ]
    for h in each:
        entry_ref[0, h] = lows[h]
        inverse_ref[0, h] = inverses[h]
        memory_ref[h] = grows[h][SPAN - 1 : SPAN, :] * memories[h] + updates[h]
        cols = slice(h * DV, (h + 1) * DV)
        delta = deltas[h]
        solved_ref[:, cols] = solveds[h]
        delta_ref[:, cols] = delta
        scaled = delta * lax.rsqrt(jnp.mean(delta * delta, axis=-1, keepdims=True) + 1e-05)
        gate = proj_ref[:, gate_at + h * DV : gate_at + (h + 1) * DV]
        mixed_ref[:, cols] = (scaled * gain_ref[0:1, :] * jax.nn.silu(gate)).astype(LOW)


def silu_back(values, grad):
    sig = jax.nn.sigmoid(values)
    return grad * sig * (1.0 + values * (1.0 - sig))


def fold(values):
    total = values[0:8]
    for part in range(1, values.shape[0] // 8):
        total = total + values[8 * part : 8 * part + 8]
    return total


def backward_kernel(
    heads, proj_ref, halo_ref, aux_ref, taps_ref, params_ref, gain_ref,
    delta_ref, solved_ref, inverse_ref, entry_ref, grad_ref,
    dproj_ref, dtaps_ref, dsmall_ref, dgain_ref, dmemory_ref, window_ref, later_ref,
):
    qk_cols, v_cols = heads * DK, heads * DV
    gate_at = 2 * qk_cols + v_cols
    small_at = gate_at + v_cols

    @pl.when(pl.program_id(0) == 0)
    def _():
        dmemory_ref[...] = jnp.zeros_like(dmemory_ref)
        later_ref[...] = jnp.zeros_like(later_ref)
        dtaps_ref[...] = jnp.zeros_like(dtaps_ref)
        dsmall_ref[...] = jnp.zeros_like(dsmall_ref)
        dgain_ref[...] = jnp.zeros_like(dgain_ref)

    window_ref[0:HALO, :] = halo_ref[:, 0:gate_at]
    window_ref[HALO : HALO + SPAN, :] = proj_ref[:, 0:gate_at]
    later_ref[SPAN : SPAN + HALO, :] = later_ref[0:HALO, :]
    aux = aux_ref[...]
    taps = taps_ref[...]
    small = proj_ref[:, small_at : small_at + LANES]
    rate, decay, writes = gates(small, params_ref[...])
    running, flipped, growth, tail, keep = decay_tables(decay, aux)
    row, col = grid_pair(SPAN, SPAN)
    lane = lax.broadcasted_iota(jnp.int32, (SPAN, LANES), 1)
    upper = (row <= col).astype(F32)
    behind = (row > col).astype(F32)
    dbeta_all = jnp.zeros((SPAN, LANES), F32)
    arrive_all = jnp.zeros((SPAN, LANES), F32)
    leave_all = jnp.zeros((SPAN, LANES), F32)
    direct_all = jnp.zeros((SPAN, LANES), F32)

    def conv_back(pre, grad, start, width):
        dpre = silu_back(pre, grad)
        later_ref[0:SPAN, start : start + width] = dpre
        total = taps[0:1, start : start + width] * dpre
        base = window_ref[HALO : HALO + SPAN, start : start + width]
        dtaps_ref[0:8, start : start + width] += fold(dpre * base)
        for offset in range(1, 4):
            ahead = later_ref[offset : offset + SPAN, start : start + width]
            total = total + taps[offset : offset + 1, start : start + width] * (
                ahead * aux[:, 5 + offset : 6 + offset]
            )
            shifted = window_ref[HALO - offset : HALO - offset + SPAN, start : start + width]
            dtaps_ref[8 * offset : 8 * offset + 8, start : start + width] += fold(
                dpre * (shifted * aux[:, 2 + offset : 3 + offset])
            )
        dproj_ref[:, start : start + width] = total.astype(LOW)

    each = range(heads)
    values_at = [slice(h * DV, (h + 1) * DV) for h in each]
    ddeltas = []
    for h in each:
        delta = delta_ref[:, values_at[h]]
        scale = lax.rsqrt(jnp.mean(delta * delta, axis=-1, keepdims=True) + 1e-05)
        scaled = delta * scale
        gate = proj_ref[:, gate_at + h * DV : gate_at + (h + 1) * DV]
        gsig = jax.nn.sigmoid(gate)
        dmixed = grad_ref[:, values_at[h]]
        gain = gain_ref[0:1, :]
        dproj_ref[:, gate_at + h * DV : gate_at + (h + 1) * DV] = (
            dmixed * scaled * gain * gsig * (1.0 + gate * (1.0 - gsig))
        ).astype(LOW)
        dnormed = dmixed * (gate * gsig)
        dgain_ref[...] += fold(dnormed * scaled)
        dnormed = dnormed * gain
        ddelta = scale * (
            dnormed - scaled * jnp.mean(scaled * dnormed, axis=-1, keepdims=True)
        )
        ddeltas.append(ddelta.astype(LOW))
    q_pres = [conv_in(window_ref, h * DK, DK, taps, aux) for h in each]
    k_pres = [conv_in(window_ref, qk_cols + h * DK, DK, taps, aux) for h in each]
    q_acts = [jax.nn.silu(pre) for pre in q_pres]
    k_acts = [jax.nn.silu(pre) for pre in k_pres]
    q_scales = [
        lax.rsqrt(jnp.sum(act * act, axis=-1, keepdims=True) + 1e-06) for act in q_acts
    ]
    k_scales = [
        lax.rsqrt(jnp.sum(act * act, axis=-1, keepdims=True) + 1e-06) for act in k_acts
    ]
    q_units = [act * scale for act, scale in zip(q_acts, q_scales)]
    keys = [act * scale for act, scale in zip(k_acts, k_scales)]
    queries = [unit_row * DK ** (-0.5) for unit_row in q_units]
    betas = [writes[:, heads + h : heads + h + 1] for h in each]
    grows = [growth[:, h : h + 1] for h in each]
    fades = [tail[:, h : h + 1] for h in each]
    withins = [
        jnp.exp(jnp.where(keep, running[:, h : h + 1] - flipped[h : h + 1, :], -1e30))
        for h in each
    ]
    key_lows = [key.astype(LOW) for key in keys]
    boths = [
        jnp.concatenate([query.astype(LOW), low], axis=0) for query, low in zip(queries, key_lows)
    ]
    scores = [mm_tb(both, low) for both, low in zip(boths, key_lows)]
    solveds = [solved_ref[:, values_at[h]] for h in each]
    entries = [entry_ref[0, h] for h in each]
    dmemories = [dmemory_ref[h] for h in each]
    dmemory_lows = [dmemory.astype(LOW) for dmemory in dmemories]
    leaving = [mm(low, dlow) for low, dlow in zip(key_lows, dmemory_lows)]
    dsolveds = [
        mm_ta(scores[h][:SPAN] * withins[h], ddeltas[h]) + fades[h] * leaving[h] for h in each
    ]
    dtargets = [mm_ta(inverse_ref[0, h], dsolveds[h]) for h in each]
    pairs = [
        jnp.concatenate([ddeltas[h], dtargets[h].astype(LOW)], axis=0) for h in each
    ]
    factors = [
        jnp.concatenate(
            [
                (grows[h] * queries[h]).astype(LOW),
                (-(betas[h] * grows[h]) * keys[h]).astype(LOW),
            ],
            axis=0,
        )
        for h in each
    ]
    flows = [mm_ta(factor, pair) for factor, pair in zip(factors, pairs)]
    carries = []
    for h in each:
        last = grows[h][SPAN - 1 : SPAN, :]
        carries.append(
            last * jnp.sum(dmemories[h] * entries[h].astype(F32), keepdims=True)
        )
        dmemory_ref[h] = last * dmemories[h] + flows[h]
    on_solveds = [mm_tb(pair, solved) for pair, solved in zip(pairs, solveds)]
    on_entries = [mm_tb(pair, entry) for pair, entry in zip(pairs, entries)]
    dkey_leaves = [
        fades[h] * mm_tb(solveds[h], dmemory_lows[h]) for h in each
    ]
    dscores = [on_solveds[h][:SPAN] * withins[h] for h in each]
    dsystems = [
        -on_solveds[h][SPAN:] * jnp.where(row > col, withins[h], 0.0) for h in each
    ]
    dsystem_betas = [betas[h] * dsystems[h] for h in each]
    duos = [
        jnp.concatenate([dscores[h].astype(LOW), dsystem_betas[h].astype(LOW)], axis=0)
        for h in each
    ]
    forths = [mm(duo, low) for duo, low in zip(duos, key_lows)]
    backs = [mm_ta(duo, both) for duo, both in zip(duos, boths)]
    spreads = [
        mm(upper, dscores[h] * scores[h][:SPAN] + dsystem_betas[h] * scores[h][SPAN:])
        for h in each
    ]
    for h in each:
        q_at, k_at, v_at = h * DK, qk_cols + h * DK, 2 * qk_cols + h * DV
        key, query, beta = keys[h], queries[h], betas[h]
        dquery_far = grows[h] * on_entries[h][:SPAN]
        dkey_far = grows[h] * on_entries[h][SPAN:]
        dquery = dquery_far + forths[h][:SPAN]
        dkey = forths[h][SPAN:] + backs[h] - beta * dkey_far + dkey_leaves[h]
        v_pre = conv_in(window_ref, v_at, DV, taps, aux)
        value = jax.nn.silu(v_pre)
        key_far = jnp.sum(key * dkey_far, axis=-1, keepdims=True)
        dbeta = (
            jnp.sum(dtargets[h] * value, axis=-1, keepdims=True)
            - key_far
            + jnp.sum(dsystems[h] * scores[h][SPAN:], axis=-1, keepdims=True)
        )
        arrive = jnp.sum(query * dquery_far, axis=-1, keepdims=True) - beta * key_far
        leave = jnp.sum(key * dkey_leaves[h], axis=-1, keepdims=True)
        direct = jnp.sum(spreads[h] * behind, axis=-1, keepdims=True) + carries[h]
        dbeta_all = jnp.where(lane == heads + h, dbeta, dbeta_all)
        arrive_all = jnp.where(lane == h, arrive, arrive_all)
        leave_all = jnp.where(lane == h, leave, leave_all)
        direct_all = jnp.where(lane == h, direct, direct_all)
        dq_unit = dquery * DK ** (-0.5)
        dq_act = q_scales[h] * (
            dq_unit - q_units[h] * jnp.sum(q_units[h] * dq_unit, axis=-1, keepdims=True)
        )
        dk_act = k_scales[h] * (dkey - key * jnp.sum(key * dkey, axis=-1, keepdims=True))
        conv_back(q_pres[h], dq_act, q_at, DK)
        conv_back(k_pres[h], dk_act, k_at, DK)
        conv_back(v_pre, beta * dtargets[h], v_at, DV)

    ddecay = direct_all + mm_exact(upper, arrive_all) + mm_exact(behind, leave_all)
    drate = ddecay * params_ref[0:1, :] * jax.nn.sigmoid(rate)
    dsmall_ref[0:8, :] += fold(ddecay * decay)
    dsmall_ref[8:16, :] += fold(drate)
    dproj_ref[:, small_at : small_at + LANES] = (
        drate + dbeta_all * writes * (1.0 - writes)
    ).astype(LOW)


def whole(shape):
    return pl.BlockSpec(shape, lambda step: (0,) * len(shape))


def mixer_forward(projected, aux, taps, params, gain, heads):
    rows, width = projected.shape
    v_cols = heads * DV
    conv_cols = taps.shape[1]
    blocks = rows // SPAN
    tall = SPAN // HALO
    return pl.pallas_call(
        functools.partial(forward_kernel, heads),
        grid=(blocks,),
        in_specs=[
            pl.BlockSpec((SPAN, width), lambda c: (c, 0)),
            pl.BlockSpec((HALO, width), lambda c: (jnp.maximum(c * tall - 1, 0), 0)),
            pl.BlockSpec((SPAN, LANES), lambda c: (c, 0)),
            whole(taps.shape),
            whole(params.shape),
            whole((8, DV)),
        ],
        out_specs=[
            pl.BlockSpec((SPAN, v_cols), lambda c: (c, 0)),
            pl.BlockSpec((SPAN, v_cols), lambda c: (c, 0)),
            pl.BlockSpec((SPAN, v_cols), lambda c: (c, 0)),
            pl.BlockSpec((1, heads, SPAN, SPAN), lambda c: (c, 0, 0, 0)),
            pl.BlockSpec((1, heads, DK, DV), lambda c: (c, 0, 0, 0)),
        ],
        out_shape=[
            jax.ShapeDtypeStruct((rows, v_cols), LOW),
            jax.ShapeDtypeStruct((rows, v_cols), F32),
            jax.ShapeDtypeStruct((rows, v_cols), LOW),
            jax.ShapeDtypeStruct((blocks, heads, SPAN, SPAN), LOW),
            jax.ShapeDtypeStruct((blocks, heads, DK, DV), LOW),
        ],
        scratch_shapes=[
            pltpu.VMEM((heads, DK, DV), F32),
            pltpu.VMEM((SPAN + HALO, conv_cols), F32),
        ],
        compiler_params=pltpu.CompilerParams(vmem_limit_bytes=40 << 20),
        cost_estimate=pl.CostEstimate(
            flops=rows, bytes_accessed=rows, transcendentals=0
        ),
        name="mixer_forward",
    )(projected, projected, aux, taps, params, gain)


def mixer_backward(projected, aux, taps, params, gain, saved, grad, heads):
    delta, solved, inverse, entry = saved
    rows, width = projected.shape
    v_cols = heads * DV
    conv_cols = taps.shape[1]
    blocks = rows // SPAN
    tall = SPAN // HALO
    last = blocks - 1
    return pl.pallas_call(
        functools.partial(backward_kernel, heads),
        grid=(blocks,),
        in_specs=[
            pl.BlockSpec((SPAN, width), lambda c: (last - c, 0)),
            pl.BlockSpec((HALO, width), lambda c: (jnp.maximum((last - c) * tall - 1, 0), 0)),
            pl.BlockSpec((SPAN, LANES), lambda c: (last - c, 0)),
            whole(taps.shape),
            whole(params.shape),
            whole((8, DV)),
            pl.BlockSpec((SPAN, v_cols), lambda c: (last - c, 0)),
            pl.BlockSpec((SPAN, v_cols), lambda c: (last - c, 0)),
            pl.BlockSpec((1, heads, SPAN, SPAN), lambda c: (last - c, 0, 0, 0)),
            pl.BlockSpec((1, heads, DK, DV), lambda c: (last - c, 0, 0, 0)),
            pl.BlockSpec((SPAN, v_cols), lambda c: (last - c, 0)),
        ],
        out_specs=[
            pl.BlockSpec((SPAN, width), lambda c: (last - c, 0)),
            whole((32, conv_cols)),
            whole((16, LANES)),
            whole((8, DV)),
        ],
        out_shape=[
            jax.ShapeDtypeStruct((rows, width), LOW),
            jax.ShapeDtypeStruct((32, conv_cols), F32),
            jax.ShapeDtypeStruct((16, LANES), F32),
            jax.ShapeDtypeStruct((8, DV), F32),
        ],
        scratch_shapes=[
            pltpu.VMEM((heads, DK, DV), F32),
            pltpu.VMEM((SPAN + HALO, conv_cols), F32),
            pltpu.VMEM((SPAN + HALO, conv_cols), F32),
        ],
        compiler_params=pltpu.CompilerParams(vmem_limit_bytes=48 << 20),
        cost_estimate=pl.CostEstimate(
            flops=rows, bytes_accessed=rows, transcendentals=0
        ),
        name="mixer_backward",
    )(projected, projected, aux, taps, params, gain, delta, solved, inverse, entry, grad)


def token_tables(segments):
    rows = segments.shape[0]
    seg = segments.astype(F32)
    blocked = seg.reshape(rows // SPAN, SPAN)
    ends = blocked[:, SPAN - 1]
    before = jnp.concatenate([jnp.full((1,), -1.0, F32), ends[:-1]])
    columns = [
        seg,
        (blocked == before[:, None]).astype(F32).reshape(rows),
        (blocked == ends[:, None]).astype(F32).reshape(rows),
    ]
    links = [(seg[offset:] == seg[:-offset]).astype(F32) for offset in range(1, 4)]
    columns += [jnp.pad(link, (offset, 0)) for offset, link in enumerate(links, 1)]
    columns += [jnp.pad(link, (0, offset)) for offset, link in enumerate(links, 1)]
    return jnp.pad(jnp.stack(columns, axis=1), ((0, 0), (0, LANES - len(columns))))


def rms_forward(values, gain_vec):
    scale = lax.rsqrt(jnp.mean(values * values, axis=-1, keepdims=True) + 1e-05)
    return values * scale * gain_vec


def rms_backward(values, gain_vec, grad):
    scale = lax.rsqrt(jnp.mean(values * values, axis=-1, keepdims=True) + 1e-05)
    scaled = values * scale
    inner = grad * gain_vec
    back = scale * (inner - scaled * jnp.mean(scaled * inner, axis=-1, keepdims=True))
    return back, jnp.sum(grad * scaled, axis=0)


def dot(left, right):
    return jnp.dot(left, right, preferred_element_type=F32)


def contract_rows(left, right):
    return lax.dot_general(
        left, right, (((0,), (0,)), ((), ())), preferred_element_type=F32
    )


def contract_cols(left, right):
    return lax.dot_general(
        left, right, (((1,), (1,)), ((), ())), preferred_element_type=F32
    )


def gather(rows):
    return lax.all_gather(rows, "tensor", axis=0, tiled=True)


def scatter(rows):
    return lax.psum_scatter(
        rows.astype(LOW), "tensor", scatter_dimension=0, tiled=True
    ).astype(F32)


def after(values, first):
    return lax.optimization_barrier((values, first))[0]


def make_body(parts, replicas):
    near = parts // 2
    teams = [list(range(near)), list(range(near, parts))]
    swap = [(i, i ^ 1) for i in range(parts)]
    across = [(i, (i + near) % parts) for i in range(parts)]

    def team_exchange(rows):
        if near == 2:
            return lax.ppermute(rows, "tensor", swap)
        return lax.all_gather(rows, "tensor", axis=0, tiled=True, axis_index_groups=teams)

    def team_join(rows, others):
        return jnp.concatenate([rows, others], axis=0) if near == 2 else others

    def team_gather(rows):
        return team_join(rows, team_exchange(rows))

    def team_scatter(rows):
        if near == 2:
            half = rows.shape[0] // 2
            return rows[:half] + lax.ppermute(rows[half:].astype(LOW), "tensor", swap).astype(F32)
        return lax.psum_scatter(
            rows.astype(LOW), "tensor", scatter_dimension=0, tiled=True, axis_index_groups=teams
        ).astype(F32)

    def scatter_direct(rows):
        size = rows.shape[0] // parts
        place = lax.axis_index("tensor")

        def part(hop):
            index = lax.rem(place + hop, parts)
            return lax.dynamic_slice_in_dim(rows, index * size, size)

        total = part(0).astype(F32)
        for hop in range(1, parts):
            pairs = [(i, (i + hop) % parts) for i in range(parts)]
            total = total + lax.ppermute(part(hop).astype(LOW), "tensor", pairs).astype(F32)
        return total

    def own_piece(matrix):
        rows = matrix.shape[0] // replicas
        return lax.dynamic_slice_in_dim(matrix, lax.axis_index("dp") * rows, rows)

    def spread(piece):
        return lax.all_gather(piece, "dp", axis=0, tiled=True)

    def body(
        block_input,
        segment_ids,
        out_cotangent,
        norm1_gain,
        query_weight,
        key_weight,
        value_weight,
        gate_weight,
        decay_weight,
        conv_query,
        conv_key,
        conv_value,
        decay_log,
        decay_bias,
        output_gain,
        output_weight,
        norm2_gain,
        ffn_gate,
        ffn_up,
        ffn_down,
    ):
        batch_count, slice_rows, width = block_input.shape
        heads = decay_log.shape[0]
        qk_cols = query_weight.shape[1]
        v_cols = value_weight.shape[1]
        ffn_cols = ffn_gate.shape[1]
        batches = range(batch_count)
        x_rows = [block_input[b].astype(F32) for b in batches]
        cot_rows = [out_cotangent[b] for b in batches]
        first_rows = [rms_forward(x_rows[b], norm1_gain).astype(LOW) for b in batches]
        ffn_both = jnp.concatenate([ffn_gate, ffn_up], axis=1)
        proj_all = jnp.concatenate(
            [
                query_weight,
                key_weight,
                value_weight,
                gate_weight,
                decay_weight.reshape(width, 2 * heads),
                jnp.zeros((width, LANES - 2 * heads), LOW),
            ],
            axis=1,
        )
        taps = jnp.pad(
            jnp.concatenate([conv_query, conv_key, conv_value], axis=1), ((0, 4), (0, 0))
        )
        params = jnp.pad(
            jnp.stack([-jnp.exp(decay_log), decay_bias]), ((0, 6), (0, LANES - heads))
        )
        gain = jnp.broadcast_to(output_gain, (8, output_gain.shape[0]))
        aux = [token_tables(segment_ids[b]) for b in batches]

        normed, projs, mixeds, saveds, branches, cot_full = [], [], [], [], [], []
        pieces = [own_piece(ffn_both), own_piece(ffn_down)]
        far = None
        for b in batches:
            rows = first_rows[b]
            if b > 0:
                rows = after(rows, normed[b - 1])
            normed.append(gather(rows))
        pieces = [
            lax.ppermute(after(piece, proj_all), "tensor", across) for piece in pieces
        ]
        far = [spread(piece) for piece in pieces]
        cot_pairs = [team_exchange(after(rows, pieces)) for rows in cot_rows]
        cot_full = [team_join(cot_rows[b], cot_pairs[b]) for b in batches]
        for b in batches:
            rows = after(normed[b], branches[b - 1]) if b > 0 else normed[b]
            projected = dot(rows, proj_all)
            mixed, *saved = mixer_forward(projected, aux[b], taps, params, gain, heads)
            mixed = after(mixed, pieces if b == 0 else cot_pairs)
            projs.append(projected)
            mixeds.append(mixed)
            saveds.append(saved)
            branches.append(dot(mixed, output_weight).astype(LOW))
        last = branches[-1]
        branches = [scatter(rows) for rows in branches]

        near_weights, far_weights = (ffn_both, ffn_down), tuple(far)

        def ffn_half(rows, cot, weights):
            both, down = weights
            gate_up = dot(rows, both)
            gate_pre, up_pre = gate_up[:, :ffn_cols], gate_up[:, ffn_cols:]
            sig = jax.nn.sigmoid(gate_pre)
            hidden = (gate_pre * sig * up_pre).astype(LOW)
            dhidden = contract_cols(cot, down)
            dgate = dhidden * up_pre * sig * (1.0 + gate_pre * (1.0 - sig))
            dup = dhidden * (gate_pre * sig)
            return hidden, jnp.concatenate([dgate, dup], axis=1).astype(LOW)

        residuals = [None] * batch_count
        ffn_full = [None] * batch_count
        hiddens = [None] * batch_count
        dboths = [None] * batch_count
        partial_in = [None] * batch_count
        partial_out = [None] * batch_count
        dresiduals = [None] * batch_count
        dbranch = [None] * batch_count
        gain2 = []

        def enter(b, behind):
            residuals[b] = x_rows[b] + after(branches[b], behind)
            low_rows = rms_forward(residuals[b], norm2_gain).astype(LOW)
            ffn_full[b] = team_gather(low_rows)
            return low_rows

        def leave(b, behind):
            dffn = after(partial_in[b], behind)
            back, part = rms_backward(residuals[b], norm2_gain, dffn)
            gain2.append(part)
            dresiduals[b] = cot_rows[b].astype(F32) + back
            low_rows = dresiduals[b].astype(LOW)
            dbranch[b] = gather(low_rows)
            return low_rows

        def over_dp(matrix):
            return lax.psum_scatter(matrix, "dp", scatter_dimension=0, tiled=True)

        def joined(halves):
            return jnp.concatenate([jnp.concatenate(h, axis=1) for h in halves], axis=0)

        enter(0, last)
        behind = None
        for b in batches:
            rows = after(ffn_full[b], behind) if b > 0 else ffn_full[b]
            near_half = ffn_half(rows, cot_full[b], near_weights)
            if b + 1 < batch_count:
                behind = enter(b + 1, near_half)
            else:
                behind = leave(b - 1, near_half)
            far_half = ffn_half(after(ffn_full[b], behind), cot_full[b], far_weights)
            hiddens[b] = [near_half[0], far_half[0]]
            dboths[b] = [near_half[1], far_half[1]]
            if b == batch_count - 1:
                down_local = contract_rows(
                    after(jnp.concatenate(cot_full, axis=0), far_half), joined(hiddens)
                ).astype(LOW)
                near_half, far_half = after((near_half, far_half), down_local)
            dffn = contract_cols(near_half[1], ffn_both) + contract_cols(
                far_half[1], far_weights[0]
            )
            partial_in[b] = team_scatter(dffn)
            ffn_out = dot(near_half[0], ffn_down) + dot(far_half[0], far_weights[1])
            partial_out[b] = team_scatter(ffn_out)
            behind = (dffn.astype(LOW), ffn_out.astype(LOW))
        outputs = [(residuals[b] + partial_out[b]).astype(LOW) for b in batches]

        both_local = contract_rows(
            after(jnp.concatenate(ffn_full, axis=0), behind), joined(dboths)
        ).astype(LOW)
        leave(batch_count - 1, both_local)
        down_grad = over_dp(down_local)
        both_grad = over_dp(both_local)
        down_other = lax.ppermute(down_grad[:, ffn_cols:], "tensor", across)

        input_grads, gain1, dtaps, dsmall, dgain = [], [], [], [], []
        grads_out, grads_proj = [], []
        behind = both_local
        for b in batches:
            rows = after(dbranch[b], behind)
            dmixed = contract_cols(rows, output_weight)
            dproj, dt, ds, dg = mixer_backward(
                projs[b], aux[b], taps, params, gain, saveds[b], dmixed, heads
            )
            dtaps.append(dt)
            dsmall.append(ds)
            dgain.append(dg)
            dproj = after(dproj, down_other if b == 0 else dnormed)
            dnormed_low = contract_cols(dproj, proj_all).astype(LOW)
            behind = dnormed_low
            dnormed = scatter_direct(dnormed_low)
            back, part = rms_backward(x_rows[b], norm1_gain, dnormed)
            gain1.append(part)
            input_grads.append((dresiduals[b] + back).astype(LOW))
            grads_proj.append((normed[b], dproj))
            grads_out.append((mixeds[b], rows))
        total_out = sum(contract_rows(after(left, behind), right) for left, right in grads_out)
        total_proj = sum(contract_rows(after(left, behind), right) for left, right in grads_proj)
        both_other = lax.ppermute(
            both_grad[:, 2 * ffn_cols :], "tensor", across
        )
        total_proj = after(total_proj.astype(LOW), both_other)
        down_grad = spread(down_grad[:, :ffn_cols] + down_other)
        both_grad = spread(both_grad[:, : 2 * ffn_cols] + both_other)
        sum_out, sum_proj = lax.psum((total_out.astype(LOW), total_proj), "dp")
        sum_taps = sum(dtaps).reshape(4, 8, -1).sum(axis=1)
        sum_small = sum(dsmall).reshape(2, 8, LANES).sum(axis=1)[:, :heads]
        sum_taps, sum_small = lax.psum((sum_taps, sum_small), "dp")
        gains = lax.psum((sum(gain1), sum(gain2), sum(dgain).sum(axis=0)), ("dp", "tensor"))
        grad_proj = sum_proj.astype(F32)
        grad_ffn = both_grad.astype(F32)
        small_at = 2 * qk_cols + 2 * v_cols
        return (
            jnp.stack(outputs, axis=0),
            jnp.stack(input_grads, axis=0),
            gains[0],
            grad_proj[:, :qk_cols],
            grad_proj[:, qk_cols : 2 * qk_cols],
            grad_proj[:, 2 * qk_cols : 2 * qk_cols + v_cols],
            grad_proj[:, 2 * qk_cols + v_cols : small_at],
            grad_proj[:, small_at : small_at + 2 * heads].reshape(width, 2, heads),
            sum_taps[:, :qk_cols],
            sum_taps[:, qk_cols : 2 * qk_cols],
            sum_taps[:, 2 * qk_cols :],
            sum_small[0],
            sum_small[1],
            gains[2],
            sum_out.astype(F32),
            gains[1],
            grad_ffn[:, :ffn_cols],
            grad_ffn[:, ffn_cols:],
            jnp.transpose(down_grad).astype(F32),
        )

    return body


def solution(mesh):
    in_specs = (
        P(None, ("dp", "tensor"), None),
        P(None, "dp"),
        P(None, ("dp", "tensor"), None),
        P(),
        P(None, "tensor"),
        P(None, "tensor"),
        P(None, "tensor"),
        P(None, "tensor"),
        P(None, None, "tensor"),
        P(None, "tensor"),
        P(None, "tensor"),
        P(None, "tensor"),
        P("tensor"),
        P("tensor"),
        P(),
        P("tensor", None),
        P(),
        P(None, "tensor"),
        P(None, "tensor"),
        P("tensor", None),
    )
    out_specs = (
        P(None, ("dp", "tensor"), None),
        P(None, ("dp", "tensor"), None),
        P(),
        P(None, "tensor"),
        P(None, "tensor"),
        P(None, "tensor"),
        P(None, "tensor"),
        P(None, None, "tensor"),
        P(None, "tensor"),
        P(None, "tensor"),
        P(None, "tensor"),
        P("tensor"),
        P("tensor"),
        P(),
        P("tensor", None),
        P(),
        P(None, "tensor"),
        P(None, "tensor"),
        P("tensor", None),
    )
    body = make_body(mesh.shape["tensor"], mesh.shape["dp"])
    return jax.shard_map(
        body, mesh=mesh, in_specs=in_specs, out_specs=out_specs, check_vma=False
    )
```
